512 devices in a mesh: tile: 128 (over z, y, core), fft: 4 (over x).
Axes of the slice: x: 4, y: 8, z: 8, core: 2. Of those that a mesh axis runs over, the one named last changes fastest.
Arguments:
- residual_sky_tiles: float32 [4096, 128, 128], P(('tile', 'fft')), may hold values from -6 to 6
- cover: int32 [128, 256], replicated, may hold values from -1 to 4095, as said below
- beam_width: float32 [128], replicated, may hold values from 1 to 2
- transfer: bfloat16 [2048, 2048], P('fft'), may hold values from 0.049804688 to 1
Outputs:
- gradient: float32 [4096, 128, 128], P(('tile', 'fft'))
The draws below stay inside these ranges and needn't reach their ends.
Inputs may be any that keep to these rules, and one draw needn't show every extreme that they name: `cover`: pointing p covers the 16 x 16 block of sky map tiles with its corner at some tile row and column; entry i * 16 + j names the tile at sky map row r = corner row + i and column c = corner column + j, or is -1 where r is outside 0 to 63 or c outside 0 to 63. Tile (r, c) has id ((c mod 16) + 16 * (r mod 32)) * 8 + (r div 32) * 4 + c div 16. Every pointing names at least one tile; pointing 0 has its corner at row 0, column 0. No pointing names more than 1 tiles whose ids share the same value of id div 8, and pointing 0 names exactly 1 such tiles.
All inputs are finite; a program needn't handle non-finite values.
Results may differ from the reference program's by a relative error of at most 0.01.
Values may be sent and summed in bfloat16 or wider, within the bound.
A program may use at most 64 MiB of HBM per device.

```python
import math
import jax
import jax.numpy as jnp
from jax import lax

L = 2048
PT = 16
FA = 64
CW = 4
TILE_PIXEL_SIDE = 128
RL = 32
MX = 64
MY = 64
MT_DEV = 8
MAP_TILE_COUNT = 4096
NP = 128


def draw_cover(key, part):
    key = jax.random.fold_in(key, 11)
    key_row, key_col = jax.random.split(key)
    row_low = min(0, MY - PT) - 2
    row_high = max(0, MY - PT) + min(3, MY)
    col_low = min(0, MX - PT) - 2
    col_high = max(0, MX - PT) + min(3, MX)
    corner_rows = jax.random.randint(key_row, (NP,), row_low, row_high)
    corner_cols = jax.random.randint(key_col, (NP,), col_low, col_high)
    first_one = jnp.arange(NP) == 0
    corner_rows = jnp.where(first_one, 0, corner_rows)
    corner_cols = jnp.where(first_one, 0, corner_cols)
    offsets = jnp.arange(PT)
    tile_rows = corner_rows[:, None, None] + offsets[None, :, None]
    tile_cols = corner_cols[:, None, None] + offsets[None, None, :]
    inside = (tile_rows >= 0) & (tile_rows < MY) & (tile_cols >= 0) & (tile_cols < MX)
    rows_safe = jnp.clip(tile_rows, 0, MY - 1)
    cols_safe = jnp.clip(tile_cols, 0, MX - 1)
    holder = cols_safe % PT + PT * (rows_safe % RL)
    local_ids = rows_safe // RL * CW + cols_safe // PT
    tile_ids = holder * MT_DEV + local_ids
    return jnp.where(inside, tile_ids, -1).reshape(NP, PT * PT).astype(jnp.int32)


def block_levels(stream_key, dims, shards, low, largest):
    factor_of = 1.0
    for axis_at, blocks in shards:
        heights = jax.random.uniform(jax.random.fold_in(jax.random.fold_in(stream_key, 6), axis_at), (blocks,), jnp.float32, low / len(shards), largest / len(shards))
        factor_of = factor_of * jnp.repeat(jnp.exp(heights), dims[axis_at] // blocks).reshape((-1,) + (1,) * (len(dims) - 1 - axis_at))
    return factor_of


def centred(own_key, extent, width, limit, shards=(), held_as=jnp.bfloat16):
    array = jax.random.normal(own_key, extent, jnp.float32) * width
    if len(shards) > 0:
        array = block_levels(own_key, extent, shards, -0.22, 0.18) * array
    return jnp.clip(array, min=-limit, max=limit).astype(held_as)


def setup_inputs(seed: int = 0) -> dict:
    seeds = jax.random.split(jax.random.key(seed), 5)
    return {
        "residual_sky_tiles": centred(seeds[0], (MAP_TILE_COUNT, TILE_PIXEL_SIDE, TILE_PIXEL_SIDE), 1.0, 6.0, ((0, 512),), jnp.float32),
        "cover": draw_cover(jax.random.fold_in(seeds[4], 71), 0),
        "beam_width": jnp.clip(jnp.exp(jax.random.uniform(seeds[2], (NP,), jnp.float32, math.log(1.0), math.log(2.0))), 1.0, 2.0),
        "transfer": jnp.clip(jnp.exp(math.log(1.0) - 2.9996462 * jax.random.uniform(seeds[3], (L, L), jnp.float32) ** block_levels(seeds[3], (L, L), ((0, 4),), -0.2, 0.2)), 0.049804688, 1.0).astype(jnp.bfloat16),
    }


def make_tables(first_len, second):
    total_len = first_len * second
    first_ids = jnp.arange(first_len, dtype=jnp.int32)
    second_ids = jnp.arange(second, dtype=jnp.int32)
    sample_ids = second_ids[:, None] + second * first_ids[None, :]
    prod_one = (sample_ids[:, :, None] * first_ids[None, None, :]) % total_len
    angle_one = (2.0 * math.pi / total_len) * prod_one.astype(jnp.float32)
    table_one = jnp.stack([jnp.cos(angle_one), -jnp.sin(angle_one)], axis=2).astype(jnp.bfloat16)
    prod_two = (second_ids[:, None] * second_ids[None, :]) % second
    angle_two = (2.0 * math.pi / second) * prod_two.astype(jnp.float32)
    cos_two = jnp.cos(angle_two)
    sin_two = jnp.sin(angle_two)
    table_two = jnp.stack([cos_two + sin_two, sin_two - cos_two], axis=0).astype(jnp.bfloat16)
    return table_one, table_two


def hartley(field_in, tables_all):
    table_one, table_two = tables_all
    second = table_one.shape[0]
    first_len = table_one.shape[1]
    columns = field_in.shape[1]
    shaped = field_in.reshape(first_len, second, columns).astype(jnp.float32)
    section_two = jnp.einsum("mra,rmtk->rtka", shaped, table_one.astype(jnp.float32), precision=lax.Precision.HIGHEST).astype(jnp.bfloat16)
    result = jnp.einsum("rtka,trj->jka", section_two.astype(jnp.float32), table_two.astype(jnp.float32), precision=lax.Precision.HIGHEST)
    return result.reshape(first_len * second, columns)


def hartley_last(field_in, tables_all):
    table_one, table_two = tables_all
    second = table_one.shape[0]
    first_len = table_one.shape[1]
    rows = field_in.shape[0]
    shaped = field_in.reshape(rows, first_len, second).astype(jnp.float32)
    section_two = jnp.einsum("amr,rmtk->rtka", shaped, table_one.astype(jnp.float32), precision=lax.Precision.HIGHEST).astype(jnp.bfloat16)
    result = jnp.einsum("rtka,trj->ajk", section_two.astype(jnp.float32), table_two.astype(jnp.float32), precision=lax.Precision.HIGHEST)
    return result.reshape(rows, first_len * second)


def reference(residual_sky_tiles, cover, beam_width, transfer):
    tile_side = residual_sky_tiles.shape[1]
    image_side = tile_side * PT
    tables_all = make_tables(FA, image_side // FA)
    tiles_bf = residual_sky_tiles.astype(jnp.bfloat16)
    coords = jnp.arange(image_side, dtype=jnp.float32) - (image_side - 1) / 2.0
    coord_sq = coords * coords
    transfer_full = transfer.astype(jnp.float32)

    def one_pointing(gradient, point_index):
        tile_ids = cover[point_index]
        is_live = tile_ids >= 0
        safe_ids = jnp.where(is_live, tile_ids, 0).astype(jnp.int32)
        blocks = jnp.where(is_live[:, None, None], tiles_bf[safe_ids], jnp.zeros((), jnp.bfloat16))
        image_full = blocks.reshape(PT, PT, tile_side, tile_side).transpose(0, 2, 1, 3).reshape(image_side, image_side)
        fwhm_frac = beam_width[point_index]
        factor = jnp.exp(-4.0 * math.log(2.0) * coord_sq / (fwhm_frac * image_side) ** 2)
        beam_map = factor[:, None] * factor[None, :]
        weighted = (beam_map * image_full.astype(jnp.float32)).astype(jnp.bfloat16)
        rowwise = hartley(weighted, tables_all).astype(jnp.bfloat16)
        spectrum = hartley_last(rowwise, tables_all).astype(jnp.bfloat16)
        filtered = (transfer_full * spectrum.astype(jnp.float32)).astype(jnp.bfloat16)
        back_cols = hartley_last(filtered, tables_all).astype(jnp.bfloat16)
        smeared = hartley(back_cols, tables_all)
        contribution = (beam_map * smeared / (image_side * image_side)).astype(jnp.bfloat16)
        pieces = contribution.reshape(PT, tile_side, PT, tile_side).transpose(0, 2, 1, 3).reshape(PT * PT, tile_side, tile_side)
        pieces = jnp.where(is_live[:, None, None], pieces.astype(jnp.float32), jnp.zeros((), jnp.float32))
        return gradient.at[safe_ids].add(pieces), None

    start = jnp.zeros(residual_sky_tiles.shape, jnp.float32)
    gradient, _ = lax.scan(one_pointing, start, jnp.arange(NP, dtype=jnp.int32))
    return gradient
```

```python
import math

import jax
import jax.numpy as jnp
import ml_dtypes
import numpy as np
from jax import lax
from jax.experimental import pallas as pl
from jax.experimental.pallas import tpu as pltpu
from jax.sharding import Mesh
from jax.sharding import PartitionSpec as P

PT = 16
ROWS = 64
COLS = 64
SIDE = 128
L = 2048
SLAB = 512
HALF = 256
HELD = 8
RELAY_X = True
RELAY_Y = True
MESH = pl.DeviceIdType.MESH
BF = jnp.bfloat16
F32 = jnp.float32


def hartley_matrix(length):
    ids = np.arange(length, dtype=np.int64)
    angle = 2.0 * np.pi / length * ((ids[:, None] * ids[None, :]) % length)
    return (np.cos(angle) + np.sin(angle)).astype(np.float32).astype(ml_dtypes.bfloat16)


def corners(cover, tiles_held):
    live = cover >= 0
    holder = cover // tiles_held
    local = cover % tiles_held
    rows = holder // PT + 32 * (local // 4)
    cols = holder % PT + PT * (local % 4)
    position = jnp.arange(PT * PT, dtype=jnp.int32)
    row_at = jnp.max(jnp.where(live, rows - position // PT, -1000), axis=1)
    col_at = jnp.max(jnp.where(live, cols - position % PT, -1000), axis=1)
    return row_at, col_at


def wait_bytes(ref, sem):
    pltpu.make_async_copy(ref, ref, sem).wait()


def kernel(
    row_at, col_at, width, sky, t_hbm, tcol_hbm, transfer_hbm, out,
    tv, tcol, trv, row_beam, col_beam, sel, p0, p1, p2, p3, send, img0, img1, w, rowsend, turned, a, spec, filt,
    backsend, ret, csend, grecv, part, rss, rsr, xrel, yrel, crel,
    load_sem, ag_send, ag_recv, y_send, y_recv, x_send, x_recv, b_send, b_recv, c_send, c_recv, rs_send, rs_recv,
    xr_recv, xf_send, yr_recv, yf_send, cr_recv, cf_send,
):
    z, y = lax.axis_index("z"), lax.axis_index("y")
    core, x = lax.axis_index("core"), lax.axis_index("fft")
    me16 = y * 2 + core
    yhi = lax.div(y, 2)
    odd = lax.rem(y, 2)
    far_y = lax.rem(y + 4, 8)
    col_class = x + 4 * core + 8 * odd
    up = {"z": lax.rem(z + 1, 8)}
    down = {"z": lax.rem(z + 7, 8)}
    pairs = [p0, p1, p2, p3]
    images = [img0, img1]
    order_in = (2, 1, 3, 0)
    order_out = (0, 1, 3, 2)

    def remote(src, dst, s_sem, r_sem, where):
        return pltpu.make_async_remote_copy(
            src_ref=src, dst_ref=dst, send_sem=s_sem, recv_sem=r_sem, device_id=where, device_id_type=MESH
        )

    def tile_index(delta, d):
        row, col = row_at[z * 16 + d], col_at[z * 16 + d]
        sky_row = row + lax.rem(yhi + 4 * lax.rem(z + delta, 4) - row + 1024, 16)
        sky_col = col + lax.rem(col_class - col + 1024, 16)
        live = (sky_row >= 0) & (sky_row < ROWS) & (sky_col >= 0) & (sky_col < COLS)
        which = lax.div(lax.rem(lax.div(sky_row, 4) - z - delta + 64, 8), 4)
        return jnp.where(live, which * 8 + lax.div(sky_row, 32) * 4 + lax.div(sky_col, 16), 16)

    load_t = pltpu.make_async_copy(t_hbm, tv, load_sem.at[0])
    load_tr = pltpu.make_async_copy(transfer_hbm, trv, load_sem.at[1])
    load_tcol = pltpu.make_async_copy(tcol_hbm, tcol, load_sem.at[2])

    barrier = pltpu.get_barrier_semaphore()
    pl.semaphore_signal(barrier, inc=1, device_id=up, device_id_type=MESH)
    pl.semaphore_signal(barrier, inc=1, device_id=down, device_id_type=MESH)

    @pl.loop(1, 16)
    def _(step):
        d = lax.rem(me16 + step, 16)
        pl.semaphore_signal(
            barrier, inc=1, device_id={"y": lax.div(d, 2), "core": lax.rem(d, 2)}, device_id_type=MESH
        )

    for step in range(1, 4):
        pl.semaphore_signal(barrier, inc=1, device_id={"fft": lax.rem(x + step, 4)}, device_id_type=MESH)
    load_t.start()
    load_tr.start()
    load_tcol.start()
    p0[0:8] = sky[...].astype(BF)
    for pair in pairs:
        pair[16] = jnp.zeros((SIDE, SIDE), BF)
    pl.semaphore_wait(barrier, 20)

    ring = [
        [(p0.at[0:8], p1.at[0:8], down), (p0.at[0:8], p3.at[8:16], up)],
        [(p1.at[0:8], p2.at[0:8], down), (p3.at[8:16], p2.at[8:16], up)],
        [(p2.at[0:8], p3.at[0:8], down), (p2.at[8:16], p1.at[8:16], up)],
        [(p3.at[0:4], p0.at[8:12], down), (p1.at[12:16], p0.at[12:16], up)],
    ]

    def ring_copies(step):
        return [
            remote(src, dst, ag_send.at[2 * step + way], ag_recv.at[2 * step + way], to)
            for way, (src, dst, to) in enumerate(ring[step])
        ]

    def stage(delta):
        pair = pairs[delta]

        @pl.loop(0, 16)
        def _(d):
            send[delta, d] = pair[tile_index(delta, d)]

    def push(delta, half):
        m = lax.rem(z + delta, 4)
        dst = images[half].at[m * 4 + yhi, core]
        r_sem = y_recv.at[half, delta]
        if RELAY_Y:
            for way in range(2):
                to = {"y": lax.rem(y + 1 + 6 * way, 8)}
                remote(
                    send.at[delta, far_y * 2 + way], yrel.at[delta, way], y_send.at[delta], yr_recv.at[delta, way], to
                ).start()

        @pl.loop(1, 16)
        def _(step):
            d = lax.rem(me16 + step, 16)
            to = {"y": lax.div(d, 2), "core": lax.rem(d, 2)}
            direct = remote(send.at[delta, d], dst, y_send.at[delta], r_sem, to)
            if RELAY_Y:
                pl.when(lax.div(d, 2) != far_y)(direct.start)
            else:
                direct.start()

        pltpu.make_async_copy(send.at[delta, me16], dst, r_sem).start()

    def forward_tile(delta, half):
        m = lax.rem(z + delta, 4)
        for way in range(2):
            source = lax.rem(y + 7 - 6 * way, 8)
            to = {"y": lax.rem(y + 3 + 2 * way, 8), "core": way}
            dst = images[half].at[m * 4 + lax.div(source, 2), core]
            wait_bytes(yrel.at[delta, way], yr_recv.at[delta, way])
            remote(yrel.at[delta, way], dst, yf_send, y_recv.at[half, delta], to).start()

    started = []
    for step in range(4):
        now = ring_copies(step)
        for copy in now:
            copy.start()
        started += now
        ready = {2: (2,), 3: (1, 3)}.get(step, ())
        for delta in ready:
            stage(delta)

            @pl.when(odd == 0)
            def _():
                push(delta, 0)

        for copy in now:
            copy.wait_recv()
    stage(0)

    @pl.when(odd == 0)
    def _():
        push(0, 0)

    center = (L - 1) / 2.0
    point = z * 16 + me16
    row_turn = lax.rem(row_at[point] + 1024, 16)
    col_turn = lax.rem(col_at[point] + 1024, 16)
    span = jnp.full((SIDE, SIDE), width[point], F32) * L
    rate = (-4.0 * math.log(2.0)) / (span * span)

    @pl.loop(0, 16)
    def _(i):
        coord = (i * SIDE + lax.broadcasted_iota(jnp.int32, (SIDE, SIDE), 0)).astype(F32) - center
        row_beam[i] = jnp.exp(rate * (coord * coord))

    for s in range(4):
        block = lax.rem(x + 4 * s + 16 - col_turn, 16)
        coord = (block * SIDE + lax.broadcasted_iota(jnp.int32, (8, SIDE), 1)).astype(F32) - center
        col_beam[:, s * SIDE : (s + 1) * SIDE] = jnp.exp(rate[0:8] * (coord * coord))

    @pl.loop(0, 4)
    def _(delta):
        lane = lax.broadcasted_iota(jnp.int32, (8, 256), 1)

        def place(p, acc):
            inside = (lane >= 16 * p) & (lane < 16 * p + 16)
            return jnp.where(inside, tile_index(delta, p) * 16 + lane - 16 * p, acc)

        target = lax.fori_loop(0, 16, place, jnp.zeros((8, 256), jnp.int32))
        row = lax.broadcasted_iota(jnp.int32, (256, 256), 0)
        sel[delta] = jnp.where(row == target[0:1], 1.0, 0.0).astype(BF)

    load_t.wait()
    load_tr.wait()
    load_tcol.wait()

    def wait_chunk(half, delta):
        wait_bytes(images[half].at[0:4], y_recv.at[half, delta])

    def weigh(half):
        image = images[half]

        @pl.loop(0, 16)
        def _(i):
            rc = lax.rem(i + row_turn, 16)
            rows = pl.ds(i * SIDE, SIDE)
            for c in range(2):
                s = c + 2 * half
                beam = row_beam[i] * col_beam[0:1, s * SIDE : (s + 1) * SIDE]
                tile = image[rc, c].astype(F32)
                w[half, rows, c * SIDE : (c + 1) * SIDE] = (beam * tile).astype(BF)

    def deliver(blocks, home, s_sem, r_sem, r_sems, stops, rel, xd):
        if RELAY_X:

            @pl.when((rel == 1) | (rel == 3))
            def _():
                for c in range(2):
                    remote(blocks[c], home[c], s_sem, r_sem, {"fft": xd}).start()

            @pl.when(rel == 2)
            def _():
                for c in range(2):
                    to = {"fft": lax.rem(x + 1 + 2 * c, 4)}
                    remote(blocks[c], stops[c], s_sem, r_sems.at[c], to).start()

        else:

            @pl.when(rel != 0)
            def _():
                for c in range(2):
                    remote(blocks[c], home[c], s_sem, r_sem, {"fft": xd}).start()

        @pl.when(rel == 0)
        def _():
            for c in range(2):
                pltpu.make_async_copy(blocks[c], home[c], r_sem).start()

    def pass_blocks(stops, homes, f_sem, r_sem, r_sems):
        if RELAY_X:
            for c in range(2):
                wait_bytes(stops[c], r_sems.at[c])
                remote(stops[c], homes[c], f_sem, r_sem, {"fft": lax.rem(x + 1 + 2 * c, 4)}).start()

    def row_transform(half):
        stops = [xrel.at[0, half, c] for c in range(2)]

        @pl.loop(0, 4)
        def _(t):
            rel = lax.rem(2 + t + lax.div(t, 2) + 2 * lax.div(t, 3), 4)
            xd = lax.rem(x + rel, 4)
            slab = jnp.dot(tv[pl.ds(xd * 4, 4)].reshape(SLAB, L), w[half], preferred_element_type=F32).astype(BF)
            for c in range(2):
                rowsend[half, xd, c] = slab[:, c * SIDE : (c + 1) * SIDE]
            blocks = [rowsend.at[half, xd, c] for c in range(2)]
            home = [turned.at[x + 4 * c + 8 * half] for c in range(2)]
            deliver(blocks, home, x_send.at[half], x_recv.at[half], xr_recv.at[0, half], stops, rel, xd)

        homes = [turned.at[lax.rem(x + 3 - 2 * c, 4) + 4 * c + 8 * half] for c in range(2)]
        pass_blocks(stops, homes, xf_send.at[0], x_recv.at[half], xr_recv.at[0, half])

    for at, delta in enumerate(order_in):
        if at == 3:

            @pl.when(odd == 1)
            def _():
                push(order_in[0], 1)
                push(order_in[1], 1)

        if RELAY_Y:

            @pl.when(odd == 1)
            def _():
                forward_tile(delta, 0)

        wait_chunk(0, delta)

    @pl.when(odd == 1)
    def _():
        push(order_in[2], 1)
        push(order_in[3], 1)

    weigh(0)
    row_transform(0)
    if RELAY_Y:

        @pl.when(odd == 0)
        def _():
            for delta in order_in:
                forward_tile(delta, 1)

    for delta in order_in:
        wait_chunk(1, delta)
    weigh(1)
    row_transform(1)

    for half in range(2):
        wait_bytes(turned.at[8 * half : 8 * half + 8], x_recv.at[half])
        for k in range(8):
            a[half, :, k * SIDE : (k + 1) * SIDE] = turned[8 * half + k]
        places = [lax.rem(8 * half + k + 16 - col_turn, 16) for k in range(8)]
        for n in range(4):
            cols = slice(n * SLAB, (n + 1) * SLAB)
            rhs = jnp.concatenate([tv[j, :, cols] for j in places], axis=0)
            total = jnp.dot(a[half], rhs, preferred_element_type=F32)
            if half == 0:
                spec[:, cols] = total
            else:
                spectrum = (spec[:, cols] + total).astype(BF)
                filt[:, cols] = (trv[:, cols].astype(F32) * spectrum.astype(F32)).astype(BF)

    for half in range(2):
        stops = [xrel.at[1, half, c] for c in range(2)]

        @pl.loop(0, 4)
        def _(t):
            rel = lax.rem(2 + t + lax.div(t, 2) + 2 * lax.div(t, 3), 4)
            xd = lax.rem(x + rel, 4)
            picked = [tcol[lax.rem(xd + 4 * c + 8 * half + 16 - col_turn, 16)] for c in range(2)]
            back = jnp.dot(filt[...], jnp.concatenate(picked, axis=1), preferred_element_type=F32).astype(BF)
            for c in range(2):
                backsend[half, xd, c] = back[:, c * SIDE : (c + 1) * SIDE]
            blocks = [backsend.at[half, xd, c] for c in range(2)]
            home = [ret.at[half, c, x] for c in range(2)]
            deliver(blocks, home, b_send.at[half], b_recv.at[half], xr_recv.at[1, half], stops, rel, xd)

        homes = [ret.at[half, c, lax.rem(x + 3 - 2 * c, 4)] for c in range(2)]
        pass_blocks(stops, homes, xf_send.at[1], b_recv.at[half], xr_recv.at[1, half])

    def forward_back(delta):
        for way in range(2):
            source = lax.rem(y + 7 - 6 * way, 8)
            to = {"y": lax.rem(y + 3 + 2 * way, 8), "core": way}
            wait_bytes(crel.at[delta, way], cr_recv.at[delta, way])
            remote(crel.at[delta, way], grecv.at[delta, source * 2 + core], cf_send, c_recv.at[delta], to).start()

    for turn in range(8):
        half, delta = turn // 4, order_out[turn % 4]
        if turn % 4 == 0:
            wait_bytes(ret.at[half], b_recv.at[half])
        m = lax.rem(z + delta, 4)
        places = [lax.rem(4 * m + yh + 16 - row_turn, 16) for yh in range(4)]
        lhs = jnp.concatenate([tv[i] for i in places], axis=0)
        rhs = jnp.concatenate([ret[half, c].reshape(L, SIDE) for c in range(2)], axis=1)
        smeared = jnp.dot(lhs, rhs, preferred_element_type=F32)
        for yh in range(4):
            rows = row_beam[places[yh]]
            for c in range(2):
                s = c + 2 * half
                beam = rows * col_beam[0:1, s * SIDE : (s + 1) * SIDE]
                tile = smeared[yh * SIDE : (yh + 1) * SIDE, c * SIDE : (c + 1) * SIDE]
                csend[half, delta, yh, c] = (beam * tile * (1.0 / (L * L))).astype(BF)

        @pl.loop(0, 8)
        def _(step):
            yh = lax.rem(yhi + lax.div(step, 2) + 2, 4)
            c = lax.rem(step, 2)
            yd = 2 * yh + half
            mine = jnp.logical_and(yd == y, c == core)
            far = yd == far_y
            src = csend.at[half, delta, yh, c]
            home = grecv.at[delta, me16]
            if RELAY_Y:

                @pl.when(far)
                def _():
                    to = {"y": lax.rem(y + 1 + 6 * c, 8)}
                    remote(src, crel.at[delta, c], c_send.at[half], cr_recv.at[delta, c], to).start()

                direct = jnp.logical_not(jnp.logical_or(mine, far))
            else:
                direct = jnp.logical_not(mine)

            @pl.when(direct)
            def _():
                remote(src, home, c_send.at[half], c_recv.at[delta], {"y": yd, "core": c}).start()

            @pl.when(mine)
            def _():
                pltpu.make_async_copy(src, home, c_recv.at[delta]).start()

        if RELAY_Y and 2 <= turn <= 5:

            @pl.when(odd == 1)
            def _():
                forward_back(order_out[turn - 2])

        if RELAY_Y and turn >= 6:

            @pl.when(odd == 0)
            def _():
                forward_back(order_out[turn - 6])

    if RELAY_Y:

        @pl.when(odd == 0)
        def _():
            forward_back(order_out[2])
            forward_back(order_out[3])

    def add_up(delta):
        wait_bytes(grecv.at[delta], c_recv.at[delta])

        @pl.loop(0, 8)
        def _(b):
            rows = pl.ds(b * 16, 16)
            stack = grecv[delta, :, rows, :].reshape(256, SIDE)
            total = jnp.dot(sel[delta], stack, preferred_element_type=F32)
            part[delta, :, rows, :] = total.reshape(16, 16, SIDE)

    def pass_on(step, way, value, tiles):
        k = 2 * step + way
        rss[k, tiles] = value.astype(BF)
        copy = remote(rss.at[k, tiles], rsr.at[k, tiles], rs_send.at[k], rs_recv.at[k], (up, down)[way])
        copy.start()
        return copy

    low, high, every = slice(0, 4), slice(4, 8), slice(0, 8)
    add_up(0)
    first = [pass_on(0, 0, part[0, 8:12], low), pass_on(0, 1, part[0, 12:16], high)]
    add_up(3)
    add_up(1)
    first[0].wait_recv()
    part[3, 0:4] = part[3, 0:4] + rsr[0, 0:4].astype(F32)
    second = [pass_on(1, 0, part[3, 0:8], every)]
    first[1].wait_recv()
    part[1, 12:16] = part[1, 12:16] + rsr[1, 4:8].astype(F32)
    second.append(pass_on(1, 1, part[1, 8:16], every))
    add_up(2)
    second[0].wait_recv()
    third = [pass_on(2, 0, part[2, 0:8] + rsr[2].astype(F32), every)]
    second[1].wait_recv()
    third.append(pass_on(2, 1, part[2, 8:16] + rsr[3].astype(F32), every))
    third[0].wait_recv()
    last = [pass_on(3, 0, part[1, 0:8] + rsr[4].astype(F32), every)]
    third[1].wait_recv()
    last.append(pass_on(3, 1, part[3, 8:16] + rsr[5].astype(F32), every))

    for copy in started:
        copy.wait_send()
    for delta in range(4):
        wait_bytes(send.at[delta, 0:15], y_send.at[delta])
    for half in range(2):
        wait_bytes(rowsend.at[half, 0:3], x_send.at[half])
        wait_bytes(backsend.at[half, 0:3], b_send.at[half])

        @pl.when(odd == half)
        def _():
            wait_bytes(csend.at[half, :, 0:3], c_send.at[half])
            wait_bytes(csend.at[half, :, 3, 0], c_send.at[half])

        @pl.when(odd != half)
        def _():
            wait_bytes(csend.at[half], c_send.at[half])

    if RELAY_X:
        for way in range(2):
            wait_bytes(xrel.at[way], xf_send.at[way])
    if RELAY_Y:
        wait_bytes(yrel, yf_send)
        wait_bytes(crel, cf_send)
    last[0].wait_recv()
    last[1].wait_recv()
    out[...] = part[0, 0:8] + rsr[6].astype(F32) + rsr[7].astype(F32)
    for copy in first + second + third + last:
        copy.wait_send()


def make_shards(table):
    by_rows = table.reshape(PT, SIDE, L)
    by_cols = np.ascontiguousarray(table.reshape(L, PT, SIDE).transpose(1, 0, 2))

    def shards(residual_sky_tiles, cover, beam_width, transfer):
        row_at, col_at = corners(cover, HELD)
        vmem = pl.BlockSpec(memory_space=pltpu.VMEM)
        smem = pl.BlockSpec(memory_space=pltpu.SMEM)
        anywhere = pl.BlockSpec(memory_space=pl.ANY)
        tile = (SIDE, SIDE)
        dma = pltpu.SemaphoreType.DMA
        scratch = [
            pltpu.VMEM((PT, SIDE, L), BF),
            pltpu.VMEM((PT, L, SIDE), BF),
            pltpu.VMEM((SLAB, L), BF),
            pltpu.VMEM((PT,) + tile, F32),
            pltpu.VMEM((8, SLAB), F32),
            pltpu.VMEM((4, 256, 256), BF),
            pltpu.VMEM((17,) + tile, BF),
            pltpu.VMEM((17,) + tile, BF),
            pltpu.VMEM((17,) + tile, BF),
            pltpu.VMEM((17,) + tile, BF),
            pltpu.VMEM((4, 16) + tile, BF),
            pltpu.VMEM((16, 2) + tile, BF),
            pltpu.VMEM((16, 2) + tile, BF),
            pltpu.VMEM((2, L, HALF), BF),
            pltpu.VMEM((2, 4, 2, SLAB, SIDE), BF),
            pltpu.VMEM((16, SLAB, SIDE), BF),
            pltpu.VMEM((2, SLAB, L // 2), BF),
            pltpu.VMEM((SLAB, L), F32),
            pltpu.VMEM((SLAB, L), BF),
            pltpu.VMEM((2, 4, 2, SLAB, SIDE), BF),
            pltpu.VMEM((2, 2, 4, SLAB, SIDE), BF),
            pltpu.VMEM((2, 4, 4, 2) + tile, BF),
            pltpu.VMEM((4, 16) + tile, BF),
            pltpu.VMEM((4, 16) + tile, F32),
            pltpu.VMEM((8, 8) + tile, BF),
            pltpu.VMEM((8, 8) + tile, BF),
            pltpu.VMEM((2, 2, 2, SLAB, SIDE), BF),
            pltpu.VMEM((4, 2) + tile, BF),
            pltpu.VMEM((4, 2) + tile, BF),
            dma((3,)),
            dma((8,)),
            dma((8,)),
            dma((4,)),
            dma((2, 4)),
            dma((2,)),
            dma((2,)),
            dma((2,)),
            dma((2,)),
            dma((2,)),
            dma((4,)),
            dma((8,)),
            dma((8,)),
            dma((2, 2, 2)),
            dma((2,)),
            dma((4, 2)),
            pltpu.SemaphoreType.DMA,
            dma((4, 2)),
            pltpu.SemaphoreType.DMA,
        ]
        return pl.pallas_call(
            kernel,
            out_shape=jax.ShapeDtypeStruct((HELD,) + tile, F32),
            in_specs=[smem, smem, smem, vmem, anywhere, anywhere, anywhere],
            out_specs=vmem,
            scratch_shapes=scratch,
            compiler_params=pltpu.CompilerParams(
                collective_id=0, has_side_effects=True, vmem_limit_bytes=63 * 1024 * 1024
            ),
            cost_estimate=pl.CostEstimate(flops=4 * 2 * L * L * SLAB, bytes_accessed=20 * 2**20, transcendentals=0),
        )(row_at, col_at, beam_width, residual_sky_tiles, jnp.asarray(by_rows), jnp.asarray(by_cols), transfer)

    return shards


def solution(mesh):
    split = Mesh(mesh.devices.reshape(8, 8, 2, 4), ("z", "y", "core", "fft"))
    over_all = P(("z", "y", "core", "fft"), None, None)
    return jax.shard_map(
        make_shards(hartley_matrix(L)),
        mesh=split,
        in_specs=(over_all, P(), P(), P("fft", None)),
        out_specs=over_all,
        check_vma=False,
    )
```

```python
import math

import jax
import jax.numpy as jnp
import ml_dtypes
import numpy as np
from jax import lax
from jax.experimental import pallas as pl
from jax.experimental.pallas import tpu as pltpu
from jax.sharding import Mesh
from jax.sharding import PartitionSpec as P

PT = 16
ROWS = 64
COLS = 64
SIDE = 128
L = 2048
SLAB = 512
HALF = 256
HELD = 8
SUBS = 4
MESH = pl.DeviceIdType.MESH
BF = jnp.bfloat16
F32 = jnp.float32


def hartley_matrix(length):
    ids = np.arange(length, dtype=np.int64)
    angle = 2.0 * np.pi / length * ((ids[:, None] * ids[None, :]) % length)
    return (np.cos(angle) + np.sin(angle)).astype(np.float32).astype(ml_dtypes.bfloat16)


def corners(cover, tiles_held):
    live = cover >= 0
    holder = cover // tiles_held
    local = cover % tiles_held
    rows = holder // PT + 32 * (local // 4)
    cols = holder % PT + PT * (local % 4)
    position = jnp.arange(PT * PT, dtype=jnp.int32)
    row_at = jnp.max(jnp.where(live, rows - position // PT, -1000), axis=1)
    col_at = jnp.max(jnp.where(live, cols - position % PT, -1000), axis=1)
    return row_at, col_at


def wait_bytes(ref, sem):
    pltpu.make_async_copy(ref, ref, sem).wait()


def kernel(
    row_at, col_at, width, sky, t_hbm, tcol_hbm, transfer_hbm, out,
    tv, tcol, trv, row_beam, col_beam, sel, p0, p1, p2, p3, send, img0, img1, img2, img3, w, rowsend, turned, a, spec, filt,
    backsend, ret, csend, grecv, part, rss, rsr, xrel,
    load_sem, ag_send, ag_recv, y_send, y_recv, x_send, x_recv, b_send, b_recv, c_send, c_recv, rs_send, rs_recv,
    xr_recv, xf_send,
):
    z, y = lax.axis_index("z"), lax.axis_index("y")
    core, x = lax.axis_index("core"), lax.axis_index("fft")
    me16 = y * 2 + core
    yhi = lax.div(y, 2)
    odd = lax.rem(y, 2)
    phase = core + 2 * odd
    col_class = x + 4 * core + 8 * odd
    up = {"z": lax.rem(z + 1, 8)}
    down = {"z": lax.rem(z + 7, 8)}
    pairs = [p0, p1, p2, p3]
    images = [img0, img1, img2, img3]
    order_in = (2, 1, 3, 0)
    order_out = (0, 1, 3, 2)

    def remote(src, dst, s_sem, r_sem, where):
        return pltpu.make_async_remote_copy(
            src_ref=src, dst_ref=dst, send_sem=s_sem, recv_sem=r_sem, device_id=where, device_id_type=MESH
        )

    def tile_index(delta, d):
        row, col = row_at[z * 16 + d], col_at[z * 16 + d]
        sky_row = row + lax.rem(yhi + 4 * lax.rem(z + delta, 4) - row + 1024, 16)
        sky_col = col + lax.rem(col_class - col + 1024, 16)
        live = (sky_row >= 0) & (sky_row < ROWS) & (sky_col >= 0) & (sky_col < COLS)
        which = lax.div(lax.rem(lax.div(sky_row, 4) - z - delta + 64, 8), 4)
        return jnp.where(live, which * 8 + lax.div(sky_row, 32) * 4 + lax.div(sky_col, 16), 16)

    load_t = pltpu.make_async_copy(t_hbm, tv, load_sem.at[0])
    load_tr = pltpu.make_async_copy(transfer_hbm, trv, load_sem.at[1])
    load_tcol = pltpu.make_async_copy(tcol_hbm, tcol, load_sem.at[2])

    barrier = pltpu.get_barrier_semaphore()
    pl.semaphore_signal(barrier, inc=1, device_id=up, device_id_type=MESH)
    pl.semaphore_signal(barrier, inc=1, device_id=down, device_id_type=MESH)

    @pl.loop(1, 16)
    def _(step):
        d = lax.rem(me16 + step, 16)
        pl.semaphore_signal(
            barrier, inc=1, device_id={"y": lax.div(d, 2), "core": lax.rem(d, 2)}, device_id_type=MESH
        )

    for step in range(1, 4):
        pl.semaphore_signal(barrier, inc=1, device_id={"fft": lax.rem(x + step, 4)}, device_id_type=MESH)
    load_t.start()
    load_tr.start()
    load_tcol.start()
    p0[0:8] = sky[...].astype(BF)
    for pair in pairs:
        pair[16] = jnp.zeros((SIDE, SIDE), BF)
    pl.semaphore_wait(barrier, 20)

    ring = [
        [(p0.at[0:8], p1.at[0:8], down), (p0.at[0:8], p3.at[8:16], up)],
        [(p1.at[0:8], p2.at[0:8], down), (p3.at[8:16], p2.at[8:16], up)],
        [(p2.at[0:8], p3.at[0:8], down), (p2.at[8:16], p1.at[8:16], up)],
        [(p3.at[0:4], p0.at[8:12], down), (p1.at[12:16], p0.at[12:16], up)],
    ]

    def ring_copy(step, way, sub):
        src, dst, to = ring[step][way]
        part_of = pl.ds(2 * sub if step < 3 else 2 * (sub - 2 * way), 2)
        k = (step * 2 + way) * SUBS + sub
        return remote(src.at[part_of], dst.at[part_of], ag_send.at[k], ag_recv.at[k], to)

    def stage(delta):
        pair = pairs[delta]

        @pl.loop(0, 16)
        def _(d):
            send[delta, d] = pair[tile_index(delta, d)]

    def push(delta, s):
        m = lax.rem(z + delta, 4)
        dst = images[s].at[m * 4 + yhi]
        r_sem = y_recv.at[s, delta]

        @pl.loop(1, 16)
        def _(step):
            d = lax.rem(me16 + step, 16)
            to = {"y": lax.div(d, 2), "core": lax.rem(d, 2)}
            remote(send.at[delta, d], dst, y_send.at[delta], r_sem, to).start()

        pltpu.make_async_copy(send.at[delta, me16], dst, r_sem).start()

    started = []
    for step in range(4):
        now = []
        for sub in range(SUBS):
            for way in range(2):
                if step > 0:
                    ring_copy(step - 1, way, sub).wait_recv()
                if step < 3 or sub // 2 == way:
                    copy = ring_copy(step, way, sub)
                    copy.start()
                    now.append(copy)
        started += now
        for delta in {2: (2,), 3: (1, 3)}.get(step, ()):
            stage(delta)

            @pl.when(phase == 0)
            def _():
                push(delta, 0)

    for copy in now:
        copy.wait_recv()
    stage(0)

    @pl.when(phase == 0)
    def _():
        push(0, 0)

    center = (L - 1) / 2.0
    point = z * 16 + me16
    row_turn = lax.rem(row_at[point] + 1024, 16)
    col_turn = lax.rem(col_at[point] + 1024, 16)
    span = jnp.full((SIDE, SIDE), width[point], F32) * L
    rate = (-4.0 * math.log(2.0)) / (span * span)

    @pl.loop(0, 16)
    def _(i):
        coord = (i * SIDE + lax.broadcasted_iota(jnp.int32, (SIDE, SIDE), 0)).astype(F32) - center
        row_beam[i] = jnp.exp(rate * (coord * coord))

    for s in range(4):
        block = lax.rem(x + 4 * s + 16 - col_turn, 16)
        coord = (block * SIDE + lax.broadcasted_iota(jnp.int32, (8, SIDE), 1)).astype(F32) - center
        col_beam[:, s * SIDE : (s + 1) * SIDE] = jnp.exp(rate[0:8] * (coord * coord))

    @pl.loop(0, 4)
    def _(delta):
        lane = lax.broadcasted_iota(jnp.int32, (8, 256), 1)

        def place(p, acc):
            inside = (lane >= 16 * p) & (lane < 16 * p + 16)
            return jnp.where(inside, tile_index(delta, p) * 16 + lane - 16 * p, acc)

        target = lax.fori_loop(0, 16, place, jnp.zeros((8, 256), jnp.int32))
        row = lax.broadcasted_iota(jnp.int32, (256, 256), 0)
        sel[delta] = jnp.where(row == target[0:1], 1.0, 0.0).astype(BF)

    load_t.wait()
    load_tr.wait()
    load_tcol.wait()

    def wait_chunk(s, delta):
        wait_bytes(images[s].at[0:4], y_recv.at[s, delta])

    def weigh(s):
        image = images[s]

        @pl.loop(0, 16)
        def _(i):
            rc = lax.rem(i + row_turn, 16)
            beam = row_beam[i] * col_beam[0:1, s * SIDE : (s + 1) * SIDE]
            w[s, pl.ds(i * SIDE, SIDE), :] = (beam * image[rc].astype(F32)).astype(BF)

    halves = [slice(0, HALF), slice(HALF, SLAB)]

    def deliver(block, home, stops, s_sem, r_sem, r_sems, rel, xd):
        @pl.when((rel == 1) | (rel == 3))
        def _():
            remote(block, home, s_sem, r_sem, {"fft": xd}).start()

        @pl.when(rel == 2)
        def _():
            for c in range(2):
                to = {"fft": lax.rem(x + 1 + 2 * c, 4)}
                remote(block.at[halves[c]], stops[c], s_sem, r_sems.at[c], to).start()

        @pl.when(rel == 0)
        def _():
            pltpu.make_async_copy(block, home, r_sem).start()

    def pass_blocks(stops, homes, f_sem, r_sem, r_sems):
        for c in range(2):
            wait_bytes(stops[c], r_sems.at[c])
            home = homes[c].at[halves[c]]
            remote(stops[c], home, f_sem, r_sem, {"fft": lax.rem(x + 1 + 2 * c, 4)}).start()

    sources = [lax.rem(x + 3 - 2 * c, 4) for c in range(2)]

    def row_transform(s):
        stops = [xrel.at[0, s, c] for c in range(2)]

        @pl.loop(0, 4)
        def _(t):
            rel = lax.rem(2 + t + lax.div(t, 2) + 2 * lax.div(t, 3), 4)
            xd = lax.rem(x + rel, 4)
            slab = jnp.dot(tv[pl.ds(xd * 4, 4)].reshape(SLAB, L), w[s], preferred_element_type=F32)
            rowsend[s, xd] = slab.astype(BF)
            deliver(
                rowsend.at[s, xd], turned.at[x + 4 * s], stops, x_send.at[s], x_recv.at[s], xr_recv.at[0, s], rel, xd
            )

        homes = [turned.at[source + 4 * s] for source in sources]
        pass_blocks(stops, homes, xf_send.at[0], x_recv.at[s], xr_recv.at[0, s])

    def add_spectrum(s):
        wait_bytes(turned.at[4 * s : 4 * s + 4], x_recv.at[s])
        for k in range(4):
            a[s, :, k * SIDE : (k + 1) * SIDE] = turned[4 * s + k]
        places = [lax.rem(4 * s + k + 16 - col_turn, 16) for k in range(4)]
        for n in range(4):
            cols = slice(n * SLAB, (n + 1) * SLAB)
            rhs = jnp.concatenate([tv[j, :, cols] for j in places], axis=0)
            total = jnp.dot(a[s], rhs, preferred_element_type=F32)
            if s > 0:
                total = spec[:, cols] + total
            if s < 3:
                spec[:, cols] = total
            else:
                filt[:, cols] = (trv[:, cols].astype(F32) * total.astype(BF).astype(F32)).astype(BF)

    for s in range(4):
        for at, delta in enumerate(order_in):
            if at == 3 and s < 3:

                @pl.when(phase == s + 1)
                def _():
                    push(order_in[0], s + 1)
                    push(order_in[1], s + 1)

            wait_chunk(s, delta)
        if s < 3:

            @pl.when(phase == s + 1)
            def _():
                push(order_in[2], s + 1)
                push(order_in[3], s + 1)

        weigh(s)
        row_transform(s)
        if s > 0:
            add_spectrum(s - 1)
    add_spectrum(3)

    def back_transform(s):
        stops = [xrel.at[1, s, c] for c in range(2)]

        @pl.loop(0, 4)
        def _(t):
            rel = lax.rem(2 + t + lax.div(t, 2) + 2 * lax.div(t, 3), 4)
            xd = lax.rem(x + rel, 4)
            picked = tcol[lax.rem(xd + 4 * s + 16 - col_turn, 16)]
            backsend[s, xd] = jnp.dot(filt[...], picked, preferred_element_type=F32).astype(BF)
            deliver(
                backsend.at[s, xd], ret.at[s, x], stops, b_send.at[s], b_recv.at[s], xr_recv.at[1, s], rel, xd
            )

        homes = [ret.at[s, source] for source in sources]
        pass_blocks(stops, homes, xf_send.at[1], b_recv.at[s], xr_recv.at[1, s])

    def give_back(s):
        wait_bytes(ret.at[s], b_recv.at[s])

        @pl.loop(0, 4)
        def _(turn):
            delta = turn + lax.div(turn, 2) * (5 - 2 * turn)
            m = lax.rem(z + delta, 4)
            places = [lax.rem(4 * m + yh + 16 - row_turn, 16) for yh in range(4)]
            lhs = jnp.concatenate([tv[i] for i in places], axis=0)
            smeared = jnp.dot(lhs, ret[s].reshape(L, SIDE), preferred_element_type=F32)
            for yh in range(4):
                beam = row_beam[places[yh]] * col_beam[0:1, s * SIDE : (s + 1) * SIDE]
                tile = smeared[yh * SIDE : (yh + 1) * SIDE]
                csend[s, delta, yh] = (beam * tile * (1.0 / (L * L))).astype(BF)

            @pl.loop(0, 4)
            def _(step):
                yh = lax.rem(yhi + step + 2, 4)
                yd = 2 * yh + s // 2
                mine = jnp.logical_and(yd == y, core == s % 2)
                src = csend.at[s, delta, yh]
                home = grecv.at[delta, me16]

                @pl.when(jnp.logical_not(mine))
                def _():
                    remote(src, home, c_send.at[s], c_recv.at[delta], {"y": yd, "core": s % 2}).start()

                @pl.when(mine)
                def _():
                    pltpu.make_async_copy(src, home, c_recv.at[delta]).start()

    back_transform(0)
    back_transform(1)
    give_back(0)
    back_transform(2)
    give_back(1)
    back_transform(3)
    give_back(2)
    give_back(3)

    def add_up(delta):
        wait_bytes(grecv.at[delta], c_recv.at[delta])

        @pl.loop(0, 8)
        def _(b):
            rows = pl.ds(b * 16, 16)
            stack = grecv[delta, :, rows, :].reshape(256, SIDE)
            total = jnp.dot(sel[delta], stack, preferred_element_type=F32)
            part[delta, :, rows, :] = total.reshape(16, 16, SIDE)

    def pass_on(step, way, sub, value):
        tiles = slice(2 * sub, 2 * sub + 2)
        k = 2 * step + way
        rss[k, tiles] = value.astype(BF)
        sem = k * SUBS + sub
        copy = remote(rss.at[k, tiles], rsr.at[k, tiles], rs_send.at[sem], rs_recv.at[sem], (up, down)[way])
        copy.start()
        return copy

    def landed(copies, step, way, sub):
        copies[step, way, sub].wait_recv()
        return rsr[2 * step + way, 2 * sub : 2 * sub + 2].astype(F32)

    passed = {}
    classes = [((0, 8), (0, 8)), ((3, 0), (1, 8)), ((2, 0), (2, 8)), ((1, 0), (3, 8))]
    for step in range(4):
        for delta in ((0,), (3, 1), (2,), ())[step]:
            add_up(delta)
        for sub in range(SUBS):
            for way in range(2):
                if step == 0 and sub // 2 != way:
                    continue
                delta, at = classes[step][way]
                value = part[delta, at + 2 * sub : at + 2 * sub + 2]
                if (step - 1, way, sub) in passed:
                    value = value + landed(passed, step - 1, way, sub)
                passed[step, way, sub] = pass_on(step, way, sub, value)

    for copy in started:
        copy.wait_send()
    for delta in range(4):
        wait_bytes(send.at[delta, 0:15], y_send.at[delta])
    for s in range(4):
        wait_bytes(rowsend.at[s, 0:3], x_send.at[s])
        wait_bytes(backsend.at[s, 0:3], b_send.at[s])

        @pl.when(phase == s)
        def _():
            wait_bytes(csend.at[s, :, 0:3], c_send.at[s])

        @pl.when(phase != s)
        def _():
            wait_bytes(csend.at[s], c_send.at[s])

    for way in range(2):
        wait_bytes(xrel.at[way], xf_send.at[way])
    for sub in range(SUBS):
        tiles = slice(2 * sub, 2 * sub + 2)
        out[tiles] = part[0, tiles] + landed(passed, 3, 0, sub) + landed(passed, 3, 1, sub)
    for copy in passed.values():
        copy.wait_send()


def make_shards(table):
    by_rows = table.reshape(PT, SIDE, L)
    by_cols = np.ascontiguousarray(table.reshape(L, PT, SIDE).transpose(1, 0, 2))

    def shards(residual_sky_tiles, cover, beam_width, transfer):
        row_at, col_at = corners(cover, HELD)
        vmem = pl.BlockSpec(memory_space=pltpu.VMEM)
        smem = pl.BlockSpec(memory_space=pltpu.SMEM)
        anywhere = pl.BlockSpec(memory_space=pl.ANY)
        tile = (SIDE, SIDE)
        dma = pltpu.SemaphoreType.DMA
        scratch = [
            pltpu.VMEM((PT, SIDE, L), BF),
            pltpu.VMEM((PT, L, SIDE), BF),
            pltpu.VMEM((SLAB, L), BF),
            pltpu.VMEM((PT,) + tile, F32),
            pltpu.VMEM((8, SLAB), F32),
            pltpu.VMEM((4, 256, 256), BF),
            pltpu.VMEM((17,) + tile, BF),
            pltpu.VMEM((17,) + tile, BF),
            pltpu.VMEM((17,) + tile, BF),
            pltpu.VMEM((17,) + tile, BF),
            pltpu.VMEM((4, 16) + tile, BF),
            pltpu.VMEM((16,) + tile, BF),
            pltpu.VMEM((16,) + tile, BF),
            pltpu.VMEM((16,) + tile, BF),
            pltpu.VMEM((16,) + tile, BF),
            pltpu.VMEM((4, L, SIDE), BF),
            pltpu.VMEM((4, 4, SLAB, SIDE), BF),
            pltpu.VMEM((16, SLAB, SIDE), BF),
            pltpu.VMEM((4, SLAB, SLAB), BF),
            pltpu.VMEM((SLAB, L), F32),
            pltpu.VMEM((SLAB, L), BF),
            pltpu.VMEM((4, 4, SLAB, SIDE), BF),
            pltpu.VMEM((4, 4, SLAB, SIDE), BF),
            pltpu.VMEM((4, 4, 4) + tile, BF),
            pltpu.VMEM((4, 16) + tile, BF),
            pltpu.VMEM((4, 16) + tile, F32),
            pltpu.VMEM((8, 8) + tile, BF),
            pltpu.VMEM((8, 8) + tile, BF),
            pltpu.VMEM((2, 4, 2, HALF, SIDE), BF),
            dma((3,)),
            dma((8 * SUBS,)),
            dma((8 * SUBS,)),
            dma((4,)),
            dma((4, 4)),
            dma((4,)),
            dma((4,)),
            dma((4,)),
            dma((4,)),
            dma((4,)),
            dma((4,)),
            dma((8 * SUBS,)),
            dma((8 * SUBS,)),
            dma((2, 4, 2)),
            dma((2,)),
        ]
        return pl.pallas_call(
            kernel,
            out_shape=jax.ShapeDtypeStruct((HELD,) + tile, F32),
            in_specs=[smem, smem, smem, vmem, anywhere, anywhere, anywhere],
            out_specs=vmem,
            scratch_shapes=scratch,
            compiler_params=pltpu.CompilerParams(
                collective_id=0, has_side_effects=True, vmem_limit_bytes=63 * 1024 * 1024
            ),
            cost_estimate=pl.CostEstimate(flops=4 * 2 * L * L * SLAB, bytes_accessed=20 * 2**20, transcendentals=0),
        )(row_at, col_at, beam_width, residual_sky_tiles, jnp.asarray(by_rows), jnp.asarray(by_cols), transfer)

    return shards


def solution(mesh):
    split = Mesh(mesh.devices.reshape(8, 8, 2, 4), ("z", "y", "core", "fft"))
    over_all = P(("z", "y", "core", "fft"), None, None)
    return jax.shard_map(
        make_shards(hartley_matrix(L)),
        mesh=split,
        in_specs=(over_all, P(), P(), P("fft", None)),
        out_specs=over_all,
        check_vma=False,
    )
```

```python
import math

import jax
import jax.numpy as jnp
import ml_dtypes
import numpy as np
from jax import lax
from jax.experimental import pallas as pl
from jax.experimental.pallas import tpu as pltpu
from jax.sharding import Mesh
from jax.sharding import PartitionSpec as P

PT = 16
ROWS = 64
COLS = 64
SIDE = 128
L = 2048
SLAB = 512
HALF = 256
HELD = 8
SUBS = 4
MESH = pl.DeviceIdType.MESH
BF = jnp.bfloat16
F32 = jnp.float32


def hartley_matrix(length):
    ids = np.arange(length, dtype=np.int64)
    angle = 2.0 * np.pi / length * ((ids[:, None] * ids[None, :]) % length)
    return (np.cos(angle) + np.sin(angle)).astype(np.float32).astype(ml_dtypes.bfloat16)


def corners(cover, tiles_held):
    live = cover >= 0
    holder = cover // tiles_held
    local = cover % tiles_held
    rows = holder // PT + 32 * (local // 4)
    cols = holder % PT + PT * (local % 4)
    position = jnp.arange(PT * PT, dtype=jnp.int32)
    row_at = jnp.max(jnp.where(live, rows - position // PT, -1000), axis=1)
    col_at = jnp.max(jnp.where(live, cols - position % PT, -1000), axis=1)
    return row_at, col_at


def wait_bytes(ref, sem):
    pltpu.make_async_copy(ref, ref, sem).wait()


def kernel(
    row_at, col_at, width, sky, t_hbm, tcol_hbm, transfer_hbm, out,
    tv, tcol, trv, row_beam, col_beam, sel, p0, p1, p2, p3, send, img0, img1, img2, img3, w, rowsend, turned, a, spec, filt,
    backsend, ret, csend, grecv, part, rss, rsr, xrel,
    load_sem, ag_send, ag_recv, y_send, y_recv, x_send, x_recv, b_send, b_recv, c_send, c_recv, rs_send, rs_recv,
    xr_recv, xf_send,
):
    z, y = lax.axis_index("z"), lax.axis_index("y")
    core, x = lax.axis_index("core"), lax.axis_index("fft")
    me16 = y * 2 + core
    yhi = lax.div(y, 2)
    odd = lax.rem(y, 2)
    phase = core + 2 * odd
    col_class = x + 4 * core + 8 * odd
    up = {"z": lax.rem(z + 1, 8)}
    down = {"z": lax.rem(z + 7, 8)}
    pairs = [p0, p1, p2, p3]
    images = [img0, img1, img2, img3]
    order_in = (2, 1, 3, 0)
    order_out = (0, 1, 3, 2)

    def remote(src, dst, s_sem, r_sem, where):
        return pltpu.make_async_remote_copy(
            src_ref=src, dst_ref=dst, send_sem=s_sem, recv_sem=r_sem, device_id=where, device_id_type=MESH
        )

    def tile_index(delta, d):
        row, col = row_at[z * 16 + d], col_at[z * 16 + d]
        sky_row = row + lax.rem(yhi + 4 * lax.rem(z + delta, 4) - row + 1024, 16)
        sky_col = col + lax.rem(col_class - col + 1024, 16)
        live = (sky_row >= 0) & (sky_row < ROWS) & (sky_col >= 0) & (sky_col < COLS)
        which = lax.div(lax.rem(lax.div(sky_row, 4) - z - delta + 64, 8), 4)
        return jnp.where(live, which * 8 + lax.div(sky_row, 32) * 4 + lax.div(sky_col, 16), 16)

    load_t = pltpu.make_async_copy(t_hbm, tv, load_sem.at[0])
    load_tr = pltpu.make_async_copy(transfer_hbm, trv, load_sem.at[1])
    load_tcol = pltpu.make_async_copy(tcol_hbm, tcol, load_sem.at[2])

    barrier = pltpu.get_barrier_semaphore()
    pl.semaphore_signal(barrier, inc=1, device_id=up, device_id_type=MESH)
    pl.semaphore_signal(barrier, inc=1, device_id=down, device_id_type=MESH)

    @pl.loop(1, 16)
    def _(step):
        d = lax.rem(me16 + step, 16)
        pl.semaphore_signal(
            barrier, inc=1, device_id={"y": lax.div(d, 2), "core": lax.rem(d, 2)}, device_id_type=MESH
        )

    for step in range(1, 4):
        pl.semaphore_signal(barrier, inc=1, device_id={"fft": lax.rem(x + step, 4)}, device_id_type=MESH)
    load_t.start()
    load_tr.start()
    load_tcol.start()
    p0[0:8] = sky[...].astype(BF)
    for pair in pairs:
        pair[16] = jnp.zeros((SIDE, SIDE), BF)
    pl.semaphore_wait(barrier, 20)

    ring = [
        [(p0.at[0:8], p1.at[0:8], down), (p0.at[0:8], p3.at[8:16], up)],
        [(p1.at[0:8], p2.at[0:8], down), (p3.at[8:16], p2.at[8:16], up)],
        [(p2.at[0:8], p3.at[0:8], down), (p2.at[8:16], p1.at[8:16], up)],
        [(p3.at[0:4], p0.at[8:12], down), (p1.at[12:16], p0.at[12:16], up)],
    ]

    def ring_copy(step, way, sub):
        src, dst, to = ring[step][way]
        part_of = pl.ds(2 * sub if step < 3 else 2 * (sub - 2 * way), 2)
        k = (step * 2 + way) * SUBS + sub
        return remote(src.at[part_of], dst.at[part_of], ag_send.at[k], ag_recv.at[k], to)

    def stage(delta):
        pair = pairs[delta]

        @pl.loop(0, 16)
        def _(d):
            send[delta, d] = pair[tile_index(delta, d)]

    def push(delta, s):
        m = lax.rem(z + delta, 4)
        dst = images[s].at[m * 4 + yhi]
        r_sem = y_recv.at[s, delta]

        @pl.loop(0, 8)
        def _(k):
            offset = 4 + (1 - 2 * lax.rem(k, 2)) * lax.div(k + 1, 2)
            yd = lax.rem(y + offset, 8)
            for c in range(2):
                d = 2 * yd + c

                @pl.when(d != me16)
                def _():
                    remote(send.at[delta, d], dst, y_send.at[delta], r_sem, {"y": yd, "core": c}).start()

        pltpu.make_async_copy(send.at[delta, me16], dst, r_sem).start()

    started = []
    for step in range(4):
        now = []
        for sub in range(SUBS):
            for way in range(2):
                if step > 0:
                    ring_copy(step - 1, way, sub).wait_recv()
                if step < 3 or sub // 2 == way:
                    copy = ring_copy(step, way, sub)
                    copy.start()
                    now.append(copy)
        started += now
        for delta in {2: (2,), 3: (1, 3)}.get(step, ()):
            stage(delta)

            @pl.when(phase == 0)
            def _():
                push(delta, 0)

            if delta == order_in[0]:

                @pl.when(phase == 1)
                def _():
                    push(delta, 1)

    for copy in now:
        copy.wait_recv()
    stage(0)

    @pl.when(phase == 0)
    def _():
        push(0, 0)

    center = (L - 1) / 2.0
    point = z * 16 + me16
    row_turn = lax.rem(row_at[point] + 1024, 16)
    col_turn = lax.rem(col_at[point] + 1024, 16)
    span = jnp.full((SIDE, SIDE), width[point], F32) * L
    rate = (-4.0 * math.log(2.0)) / (span * span)

    @pl.loop(0, 16)
    def _(i):
        coord = (i * SIDE + lax.broadcasted_iota(jnp.int32, (SIDE, SIDE), 0)).astype(F32) - center
        row_beam[i] = jnp.exp(rate * (coord * coord))

    for s in range(4):
        block = lax.rem(x + 4 * s + 16 - col_turn, 16)
        coord = (block * SIDE + lax.broadcasted_iota(jnp.int32, (8, SIDE), 1)).astype(F32) - center
        col_beam[:, s * SIDE : (s + 1) * SIDE] = jnp.exp(rate[0:8] * (coord * coord))

    @pl.loop(0, 4)
    def _(delta):
        lane = lax.broadcasted_iota(jnp.int32, (8, 256), 1)

        def place(p, acc):
            inside = (lane >= 16 * p) & (lane < 16 * p + 16)
            return jnp.where(inside, tile_index(delta, p) * 16 + lane - 16 * p, acc)

        target = lax.fori_loop(0, 16, place, jnp.zeros((8, 256), jnp.int32))
        row = lax.broadcasted_iota(jnp.int32, (256, 256), 0)
        sel[delta] = jnp.where(row == target[0:1], 1.0, 0.0).astype(BF)

    load_t.wait()
    load_tr.wait()
    load_tcol.wait()

    def wait_chunk(s, delta):
        wait_bytes(images[s].at[0:4], y_recv.at[s, delta])

    def weigh(s):
        image = images[s]

        @pl.loop(0, 16)
        def _(i):
            rc = lax.rem(i + row_turn, 16)
            beam = row_beam[i] * col_beam[0:1, s * SIDE : (s + 1) * SIDE]
            w[s, pl.ds(i * SIDE, SIDE), :] = (beam * image[rc].astype(F32)).astype(BF)

    halves = [slice(0, HALF), slice(HALF, SLAB)]

    def deliver(block, home, stops, s_sem, r_sem, r_sems, rel, xd):
        @pl.when((rel == 1) | (rel == 3))
        def _():
            remote(block, home, s_sem, r_sem, {"fft": xd}).start()

        @pl.when(rel == 2)
        def _():
            for c in range(2):
                to = {"fft": lax.rem(x + 1 + 2 * c, 4)}
                remote(block.at[halves[c]], stops[c], s_sem, r_sems.at[c], to).start()

        @pl.when(rel == 0)
        def _():
            pltpu.make_async_copy(block, home, r_sem).start()

    def pass_blocks(stops, homes, f_sem, r_sem, r_sems):
        for c in range(2):
            wait_bytes(stops[c], r_sems.at[c])
            home = homes[c].at[halves[c]]
            remote(stops[c], home, f_sem, r_sem, {"fft": lax.rem(x + 1 + 2 * c, 4)}).start()

    sources = [lax.rem(x + 3 - 2 * c, 4) for c in range(2)]

    def row_transform(s):
        stops = [xrel.at[0, s, c] for c in range(2)]

        @pl.loop(0, 4)
        def _(t):
            rel = lax.rem(2 + t + lax.div(t, 2) + 2 * lax.div(t, 3), 4)
            xd = lax.rem(x + rel, 4)
            slab = jnp.dot(tv[pl.ds(xd * 4, 4)].reshape(SLAB, L), w[s], preferred_element_type=F32)
            rowsend[s, xd] = slab.astype(BF)
            deliver(
                rowsend.at[s, xd], turned.at[x + 4 * s], stops, x_send.at[s], x_recv.at[s], xr_recv.at[0, s], rel, xd
            )

        homes = [turned.at[source + 4 * s] for source in sources]
        pass_blocks(stops, homes, xf_send.at[0], x_recv.at[s], xr_recv.at[0, s])

    def add_spectrum(s):
        wait_bytes(turned.at[4 * s : 4 * s + 4], x_recv.at[s])
        for k in range(4):
            a[s, :, k * SIDE : (k + 1) * SIDE] = turned[4 * s + k]
        places = [lax.rem(4 * s + k + 16 - col_turn, 16) for k in range(4)]
        for n in range(4):
            cols = slice(n * SLAB, (n + 1) * SLAB)
            rhs = jnp.concatenate([tv[j, :, cols] for j in places], axis=0)
            total = jnp.dot(a[s], rhs, preferred_element_type=F32)
            if s > 0:
                total = spec[:, cols] + total
            if s < 3:
                spec[:, cols] = total
            else:
                filt[:, cols] = (trv[:, cols].astype(F32) * total.astype(BF).astype(F32)).astype(BF)

    for s in range(4):
        for at, delta in enumerate(order_in):
            if s < 3 and (at, s) in ((2, 1), (2, 2), (3, 0), (3, 1), (3, 2)):

                @pl.when(phase == s + 1)
                def _():
                    push(order_in[1 if s == 0 else at - 2], s + 1)

            wait_chunk(s, delta)
        if s < 3:

            @pl.when(phase == s + 1)
            def _():
                push(order_in[2], s + 1)
                push(order_in[3], s + 1)

        weigh(s)
        row_transform(s)
        if s > 0:
            add_spectrum(s - 1)
    add_spectrum(3)

    def back_transform(s):
        stops = [xrel.at[1, s, c] for c in range(2)]

        @pl.loop(0, 4)
        def _(t):
            rel = lax.rem(2 + t + lax.div(t, 2) + 2 * lax.div(t, 3), 4)
            xd = lax.rem(x + rel, 4)
            picked = tcol[lax.rem(xd + 4 * s + 16 - col_turn, 16)]
            backsend[s, xd] = jnp.dot(filt[...], picked, preferred_element_type=F32).astype(BF)
            deliver(
                backsend.at[s, xd], ret.at[s, x], stops, b_send.at[s], b_recv.at[s], xr_recv.at[1, s], rel, xd
            )

        homes = [ret.at[s, source] for source in sources]
        pass_blocks(stops, homes, xf_send.at[1], b_recv.at[s], xr_recv.at[1, s])

    def give_back(s):
        wait_bytes(ret.at[s], b_recv.at[s])

        @pl.loop(0, 4)
        def _(turn):
            delta = turn + lax.div(turn, 2) * (5 - 2 * turn)
            m = lax.rem(z + delta, 4)
            places = [lax.rem(4 * m + yh + 16 - row_turn, 16) for yh in range(4)]
            lhs = jnp.concatenate([tv[i] for i in places], axis=0)
            smeared = jnp.dot(lhs, ret[s].reshape(L, SIDE), preferred_element_type=F32)
            for yh in range(4):
                beam = row_beam[places[yh]] * col_beam[0:1, s * SIDE : (s + 1) * SIDE]
                tile = smeared[yh * SIDE : (yh + 1) * SIDE]
                csend[s, delta, yh] = (beam * tile * (1.0 / (L * L))).astype(BF)

            @pl.loop(0, 4)
            def _(step):
                yh = lax.rem(yhi + step + 2, 4)
                yd = 2 * yh + s // 2
                mine = jnp.logical_and(yd == y, core == s % 2)
                src = csend.at[s, delta, yh]
                home = grecv.at[delta, me16]

                @pl.when(jnp.logical_not(mine))
                def _():
                    remote(src, home, c_send.at[s], c_recv.at[delta], {"y": yd, "core": s % 2}).start()

                @pl.when(mine)
                def _():
                    pltpu.make_async_copy(src, home, c_recv.at[delta]).start()

    back_transform(0)
    back_transform(1)
    give_back(0)
    back_transform(2)
    give_back(1)
    back_transform(3)
    give_back(2)
    give_back(3)

    def add_up(delta):
        wait_bytes(grecv.at[delta], c_recv.at[delta])

        @pl.loop(0, 8)
        def _(b):
            rows = pl.ds(b * 16, 16)
            stack = grecv[delta, :, rows, :].reshape(256, SIDE)
            total = jnp.dot(sel[delta], stack, preferred_element_type=F32)
            part[delta, :, rows, :] = total.reshape(16, 16, SIDE)

    def pass_on(step, way, sub, value):
        tiles = slice(2 * sub, 2 * sub + 2)
        k = 2 * step + way
        rss[k, tiles] = value.astype(BF)
        sem = k * SUBS + sub
        copy = remote(rss.at[k, tiles], rsr.at[k, tiles], rs_send.at[sem], rs_recv.at[sem], (up, down)[way])
        copy.start()
        return copy

    def landed(copies, step, way, sub):
        copies[step, way, sub].wait_recv()
        return rsr[2 * step + way, 2 * sub : 2 * sub + 2].astype(F32)

    passed = {}
    classes = [((0, 8), (0, 8)), ((3, 0), (1, 8)), ((2, 0), (2, 8)), ((1, 0), (3, 8))]
    for step in range(4):
        for delta in ((0,), (3, 1), (2,), ())[step]:
            add_up(delta)
        for sub in range(SUBS):
            for way in range(2):
                if step == 0 and sub // 2 != way:
                    continue
                delta, at = classes[step][way]
                value = part[delta, at + 2 * sub : at + 2 * sub + 2]
                if (step - 1, way, sub) in passed:
                    value = value + landed(passed, step - 1, way, sub)
                passed[step, way, sub] = pass_on(step, way, sub, value)

    for copy in started:
        copy.wait_send()
    for delta in range(4):
        wait_bytes(send.at[delta, 0:15], y_send.at[delta])
    for s in range(4):
        wait_bytes(rowsend.at[s, 0:3], x_send.at[s])
        wait_bytes(backsend.at[s, 0:3], b_send.at[s])

        @pl.when(phase == s)
        def _():
            wait_bytes(csend.at[s, :, 0:3], c_send.at[s])

        @pl.when(phase != s)
        def _():
            wait_bytes(csend.at[s], c_send.at[s])

    for way in range(2):
        wait_bytes(xrel.at[way], xf_send.at[way])
    for sub in range(SUBS):
        tiles = slice(2 * sub, 2 * sub + 2)
        out[tiles] = part[0, tiles] + landed(passed, 3, 0, sub) + landed(passed, 3, 1, sub)
    for copy in passed.values():
        copy.wait_send()


def make_shards(table):
    by_rows = table.reshape(PT, SIDE, L)
    by_cols = np.ascontiguousarray(table.reshape(L, PT, SIDE).transpose(1, 0, 2))

    def shards(residual_sky_tiles, cover, beam_width, transfer):
        row_at, col_at = corners(cover, HELD)
        vmem = pl.BlockSpec(memory_space=pltpu.VMEM)
        smem = pl.BlockSpec(memory_space=pltpu.SMEM)
        anywhere = pl.BlockSpec(memory_space=pl.ANY)
        tile = (SIDE, SIDE)
        dma = pltpu.SemaphoreType.DMA
        scratch = [
            pltpu.VMEM((PT, SIDE, L), BF),
            pltpu.VMEM((PT, L, SIDE), BF),
            pltpu.VMEM((SLAB, L), BF),
            pltpu.VMEM((PT,) + tile, F32),
            pltpu.VMEM((8, SLAB), F32),
            pltpu.VMEM((4, 256, 256), BF),
            pltpu.VMEM((17,) + tile, BF),
            pltpu.VMEM((17,) + tile, BF),
            pltpu.VMEM((17,) + tile, BF),
            pltpu.VMEM((17,) + tile, BF),
            pltpu.VMEM((4, 16) + tile, BF),
            pltpu.VMEM((16,) + tile, BF),
            pltpu.VMEM((16,) + tile, BF),
            pltpu.VMEM((16,) + tile, BF),
            pltpu.VMEM((16,) + tile, BF),
            pltpu.VMEM((4, L, SIDE), BF),
            pltpu.VMEM((4, 4, SLAB, SIDE), BF),
            pltpu.VMEM((16, SLAB, SIDE), BF),
            pltpu.VMEM((4, SLAB, SLAB), BF),
            pltpu.VMEM((SLAB, L), F32),
            pltpu.VMEM((SLAB, L), BF),
            pltpu.VMEM((4, 4, SLAB, SIDE), BF),
            pltpu.VMEM((4, 4, SLAB, SIDE), BF),
            pltpu.VMEM((4, 4, 4) + tile, BF),
            pltpu.VMEM((4, 16) + tile, BF),
            pltpu.VMEM((4, 16) + tile, F32),
            pltpu.VMEM((8, 8) + tile, BF),
            pltpu.VMEM((8, 8) + tile, BF),
            pltpu.VMEM((2, 4, 2, HALF, SIDE), BF),
            dma((3,)),
            dma((8 * SUBS,)),
            dma((8 * SUBS,)),
            dma((4,)),
            dma((4, 4)),
            dma((4,)),
            dma((4,)),
            dma((4,)),
            dma((4,)),
            dma((4,)),
            dma((4,)),
            dma((8 * SUBS,)),
            dma((8 * SUBS,)),
            dma((2, 4, 2)),
            dma((2,)),
        ]
        return pl.pallas_call(
            kernel,
            out_shape=jax.ShapeDtypeStruct((HELD,) + tile, F32),
            in_specs=[smem, smem, smem, vmem, anywhere, anywhere, anywhere],
            out_specs=vmem,
            scratch_shapes=scratch,
            compiler_params=pltpu.CompilerParams(
                collective_id=0, has_side_effects=True, vmem_limit_bytes=63 * 1024 * 1024
            ),
            cost_estimate=pl.CostEstimate(flops=4 * 2 * L * L * SLAB, bytes_accessed=20 * 2**20, transcendentals=0),
        )(row_at, col_at, beam_width, residual_sky_tiles, jnp.asarray(by_rows), jnp.asarray(by_cols), transfer)

    return shards


def solution(mesh):
    split = Mesh(mesh.devices.reshape(8, 8, 2, 4), ("z", "y", "core", "fft"))
    over_all = P(("z", "y", "core", "fft"), None, None)
    return jax.shard_map(
        make_shards(hartley_matrix(L)),
        mesh=split,
        in_specs=(over_all, P(), P(), P("fft", None)),
        out_specs=over_all,
        check_vma=False,
    )
```

```python
import math

import jax
import jax.numpy as jnp
import ml_dtypes
import numpy as np
from jax import lax
from jax.experimental import pallas as pl
from jax.experimental.pallas import tpu as pltpu
from jax.sharding import Mesh
from jax.sharding import PartitionSpec as P

PT = 16
ROWS = 64
COLS = 64
SIDE = 128
L = 2048
SLAB = 512
HALF = 256
HELD = 8
SUBS = 4
MESH = pl.DeviceIdType.MESH
BF = jnp.bfloat16
F32 = jnp.float32


def hartley_matrix(length):
    ids = np.arange(length, dtype=np.int64)
    angle = 2.0 * np.pi / length * ((ids[:, None] * ids[None, :]) % length)
    return (np.cos(angle) + np.sin(angle)).astype(np.float32).astype(ml_dtypes.bfloat16)


def corners(cover, tiles_held):
    live = cover >= 0
    holder = cover // tiles_held
    local = cover % tiles_held
    rows = holder // PT + 32 * (local // 4)
    cols = holder % PT + PT * (local % 4)
    position = jnp.arange(PT * PT, dtype=jnp.int32)
    row_at = jnp.max(jnp.where(live, rows - position // PT, -1000), axis=1)
    col_at = jnp.max(jnp.where(live, cols - position % PT, -1000), axis=1)
    return row_at, col_at


def wait_bytes(ref, sem):
    pltpu.make_async_copy(ref, ref, sem).wait()


def kernel(
    row_at, col_at, width, sky, t_hbm, tcol_hbm, transfer_hbm, out,
    tv, tcol, trv, row_beam, col_beam, sel, p0, p1, p2, p3, send, img0, img1, img2, img3, w, rowsend, turned, a, spec, filt,
    backsend, ret, csend, grecv, part, rss, rsr, xrel,
    load_sem, ag_send, ag_recv, y_send, y_recv, x_send, x_recv, b_send, b_recv, c_send, c_recv, rs_send, rs_recv,
    xr_recv, xf_send,
):
    z, y = lax.axis_index("z"), lax.axis_index("y")
    core, x = lax.axis_index("core"), lax.axis_index("fft")
    me16 = y * 2 + core
    yhi = lax.div(y, 2)
    odd = lax.rem(y, 2)
    phase = core + 2 * odd
    col_class = x + 4 * core + 8 * odd
    up = {"z": lax.rem(z + 1, 8)}
    down = {"z": lax.rem(z + 7, 8)}
    pairs = [p0, p1, p2, p3]
    images = [img0, img1, img2, img3]
    order_in = (2, 1, 3, 0)
    order_out = (0, 1, 3, 2)

    def remote(src, dst, s_sem, r_sem, where):
        return pltpu.make_async_remote_copy(
            src_ref=src, dst_ref=dst, send_sem=s_sem, recv_sem=r_sem, device_id=where, device_id_type=MESH
        )

    def tile_index(delta, d):
        row, col = row_at[z * 16 + d], col_at[z * 16 + d]
        sky_row = row + lax.rem(yhi + 4 * lax.rem(z + delta, 4) - row + 1024, 16)
        sky_col = col + lax.rem(col_class - col + 1024, 16)
        live = (sky_row >= 0) & (sky_row < ROWS) & (sky_col >= 0) & (sky_col < COLS)
        which = lax.div(lax.rem(lax.div(sky_row, 4) - z - delta + 64, 8), 4)
        return jnp.where(live, which * 8 + lax.div(sky_row, 32) * 4 + lax.div(sky_col, 16), 16)

    load_t = pltpu.make_async_copy(t_hbm, tv, load_sem.at[0])
    load_tr = pltpu.make_async_copy(transfer_hbm, trv, load_sem.at[1])
    load_tcol = pltpu.make_async_copy(tcol_hbm, tcol, load_sem.at[2])

    barrier = pltpu.get_barrier_semaphore()
    pl.semaphore_signal(barrier, inc=1, device_id=up, device_id_type=MESH)
    pl.semaphore_signal(barrier, inc=1, device_id=down, device_id_type=MESH)

    @pl.loop(1, 16)
    def _(step):
        d = lax.rem(me16 + step, 16)
        pl.semaphore_signal(
            barrier, inc=1, device_id={"y": lax.div(d, 2), "core": lax.rem(d, 2)}, device_id_type=MESH
        )

    for step in range(1, 4):
        pl.semaphore_signal(barrier, inc=1, device_id={"fft": lax.rem(x + step, 4)}, device_id_type=MESH)
    load_t.start()
    load_tr.start()
    load_tcol.start()
    p0[0:8] = sky[...].astype(BF)
    for pair in pairs:
        pair[16] = jnp.zeros((SIDE, SIDE), BF)
    pl.semaphore_wait(barrier, 20)

    ring = [
        [(p0.at[0:8], p1.at[0:8], down), (p0.at[0:8], p3.at[8:16], up)],
        [(p1.at[0:8], p2.at[0:8], down), (p3.at[8:16], p2.at[8:16], up)],
        [(p2.at[0:8], p3.at[0:8], down), (p2.at[8:16], p1.at[8:16], up)],
        [(p3.at[0:4], p0.at[8:12], down), (p1.at[12:16], p0.at[12:16], up)],
    ]

    def ring_copy(step, way, sub):
        src, dst, to = ring[step][way]
        part_of = pl.ds(2 * sub if step < 3 else 2 * (sub - 2 * way), 2)
        k = (step * 2 + way) * SUBS + sub
        return remote(src.at[part_of], dst.at[part_of], ag_send.at[k], ag_recv.at[k], to)

    def stage(delta):
        pair = pairs[delta]

        @pl.loop(0, 16)
        def _(d):
            send[delta, d] = pair[tile_index(delta, d)]

    def push(delta, s):
        m = lax.rem(z + delta, 4)
        dst = images[s].at[m * 4 + yhi]
        r_sem = y_recv.at[s, delta]

        @pl.loop(0, 8)
        def _(k):
            offset = 4 + (1 - 2 * lax.rem(k, 2)) * lax.div(k + 1, 2)
            yd = lax.rem(y + offset, 8)
            for c in range(2):
                d = 2 * yd + c

                @pl.when(d != me16)
                def _():
                    remote(send.at[delta, d], dst, y_send.at[delta], r_sem, {"y": yd, "core": c}).start()

        pltpu.make_async_copy(send.at[delta, me16], dst, r_sem).start()

    started = []
    for step in range(4):
        now = []
        for sub in range(SUBS):
            for way in range(2):
                if step > 0:
                    ring_copy(step - 1, way, sub).wait_recv()
                if step < 3 or sub // 2 == way:
                    copy = ring_copy(step, way, sub)
                    copy.start()
                    now.append(copy)
        started += now
        for delta in {2: (2,), 3: (1, 3)}.get(step, ()):
            stage(delta)

            @pl.when(phase == 0)
            def _():
                push(delta, 0)

            if delta == order_in[0]:

                @pl.when(phase == 1)
                def _():
                    push(delta, 1)

    for copy in now:
        copy.wait_recv()
    stage(0)

    @pl.when(phase == 0)
    def _():
        push(0, 0)

    center = (L - 1) / 2.0
    point = z * 16 + me16
    row_turn = lax.rem(row_at[point] + 1024, 16)
    col_turn = lax.rem(col_at[point] + 1024, 16)
    span = jnp.full((SIDE, SIDE), width[point], F32) * L
    rate = (-4.0 * math.log(2.0)) / (span * span)

    @pl.loop(0, 16)
    def _(i):
        coord = (i * SIDE + lax.broadcasted_iota(jnp.int32, (SIDE, SIDE), 0)).astype(F32) - center
        row_beam[i] = jnp.exp(rate * (coord * coord))

    for s in range(4):
        block = lax.rem(x + 4 * s + 16 - col_turn, 16)
        coord = (block * SIDE + lax.broadcasted_iota(jnp.int32, (8, SIDE), 1)).astype(F32) - center
        col_beam[:, s * SIDE : (s + 1) * SIDE] = jnp.exp(rate[0:8] * (coord * coord))

    @pl.loop(0, 4)
    def _(delta):
        lane = lax.broadcasted_iota(jnp.int32, (8, 256), 1)

        def place(p, acc):
            inside = (lane >= 16 * p) & (lane < 16 * p + 16)
            return jnp.where(inside, tile_index(delta, p) * 16 + lane - 16 * p, acc)

        target = lax.fori_loop(0, 16, place, jnp.zeros((8, 256), jnp.int32))
        row = lax.broadcasted_iota(jnp.int32, (256, 256), 0)
        sel[delta] = jnp.where(row == target[0:1], 1.0, 0.0).astype(BF)

    load_t.wait()
    load_tr.wait()
    load_tcol.wait()

    def wait_chunk(s, delta):
        wait_bytes(images[s].at[0:4], y_recv.at[s, delta])

    def weigh(s):
        image = images[s]

        @pl.loop(0, 16)
        def _(i):
            rc = lax.rem(i + row_turn, 16)
            beam = row_beam[i] * col_beam[0:1, s * SIDE : (s + 1) * SIDE]
            w[s, pl.ds(i * SIDE, SIDE), :] = (beam * image[rc].astype(F32)).astype(BF)

    halves = [slice(0, HALF), slice(HALF, SLAB)]

    def deliver(block, home, stops, s_sem, r_sem, r_sems, rel, xd):
        @pl.when((rel == 1) | (rel == 3))
        def _():
            remote(block, home, s_sem, r_sem, {"fft": xd}).start()

        @pl.when(rel == 2)
        def _():
            for c in range(2):
                to = {"fft": lax.rem(x + 1 + 2 * c, 4)}
                remote(block.at[halves[c]], stops[c], s_sem, r_sems.at[c], to).start()

        @pl.when(rel == 0)
        def _():
            pltpu.make_async_copy(block, home, r_sem).start()

    def pass_blocks(stops, homes, f_sem, r_sem, r_sems):
        for c in range(2):
            wait_bytes(stops[c], r_sems.at[c])
            home = homes[c].at[halves[c]]
            remote(stops[c], home, f_sem, r_sem, {"fft": lax.rem(x + 1 + 2 * c, 4)}).start()

    sources = [lax.rem(x + 3 - 2 * c, 4) for c in range(2)]

    def beside(blocks):
        return blocks[0] if len(blocks) == 1 else jnp.concatenate(blocks, axis=1)

    def row_transform(quarters):
        @pl.loop(0, 4)
        def _(t):
            rel = lax.rem(2 + t + lax.div(t, 2) + 2 * lax.div(t, 3), 4)
            xd = lax.rem(x + rel, 4)
            slab = jnp.dot(
                tv[pl.ds(xd * 4, 4)].reshape(SLAB, L), beside([w[s] for s in quarters]), preferred_element_type=F32
            ).astype(BF)
            for at, s in enumerate(quarters):
                stops = [xrel.at[0, s, c] for c in range(2)]
                rowsend[s, xd] = slab[:, at * SIDE : (at + 1) * SIDE]
                home = turned.at[x + 4 * s]
                deliver(rowsend.at[s, xd], home, stops, x_send.at[s], x_recv.at[s], xr_recv.at[0, s], rel, xd)

        for s in quarters:
            stops = [xrel.at[0, s, c] for c in range(2)]
            homes = [turned.at[source + 4 * s] for source in sources]
            pass_blocks(stops, homes, xf_send.at[0], x_recv.at[s], xr_recv.at[0, s])

    def add_spectrum(quarters):
        places = {}
        for s in quarters:
            wait_bytes(turned.at[4 * s : 4 * s + 4], x_recv.at[s])
            for k in range(4):
                a[s, :, k * SIDE : (k + 1) * SIDE] = turned[4 * s + k]
            places[s] = [lax.rem(4 * s + k + 16 - col_turn, 16) for k in range(4)]
        for n in range(4):
            cols = slice(n * SLAB, (n + 1) * SLAB)
            total = None if quarters[0] == 0 else spec[:, cols]
            for s in quarters:
                rhs = jnp.concatenate([tv[j, :, cols] for j in places[s]], axis=0)
                term = jnp.dot(a[s], rhs, preferred_element_type=F32)
                total = term if total is None else total + term
            if quarters[-1] < 3:
                spec[:, cols] = total
            else:
                filt[:, cols] = (trv[:, cols].astype(F32) * total.astype(BF).astype(F32)).astype(BF)

    for s in range(4):
        for at, delta in enumerate(order_in):
            if s < 3 and (at, s) in ((2, 1), (2, 2), (3, 0), (3, 1), (3, 2)):

                @pl.when(phase == s + 1)
                def _():
                    push(order_in[1 if s == 0 else at - 2], s + 1)

            wait_chunk(s, delta)
        if s < 3:

            @pl.when(phase == s + 1)
            def _():
                push(order_in[2], s + 1)
                push(order_in[3], s + 1)

        weigh(s)
        if s == 1:
            row_transform((0, 1))
        if s == 2:
            row_transform((2,))
            add_spectrum((0, 1))
        if s == 3:
            row_transform((3,))
            add_spectrum((2,))
    add_spectrum((3,))

    def back_transform(quarters):
        @pl.loop(0, 4)
        def _(t):
            rel = lax.rem(2 + t + lax.div(t, 2) + 2 * lax.div(t, 3), 4)
            xd = lax.rem(x + rel, 4)
            picked = beside([tcol[lax.rem(xd + 4 * s + 16 - col_turn, 16)] for s in quarters])
            back = jnp.dot(filt[...], picked, preferred_element_type=F32).astype(BF)
            for at, s in enumerate(quarters):
                stops = [xrel.at[1, s, c] for c in range(2)]
                backsend[s, xd] = back[:, at * SIDE : (at + 1) * SIDE]
                home = ret.at[s, x]
                deliver(backsend.at[s, xd], home, stops, b_send.at[s], b_recv.at[s], xr_recv.at[1, s], rel, xd)

        for s in quarters:
            stops = [xrel.at[1, s, c] for c in range(2)]
            homes = [ret.at[s, source] for source in sources]
            pass_blocks(stops, homes, xf_send.at[1], b_recv.at[s], xr_recv.at[1, s])

    def give_back(quarters):
        for s in quarters:
            wait_bytes(ret.at[s], b_recv.at[s])

        @pl.loop(0, 4)
        def _(turn):
            delta = turn + lax.div(turn, 2) * (5 - 2 * turn)
            m = lax.rem(z + delta, 4)
            places = [lax.rem(4 * m + yh + 16 - row_turn, 16) for yh in range(4)]
            lhs = jnp.concatenate([tv[i] for i in places], axis=0)
            smeared = jnp.dot(lhs, beside([ret[s].reshape(L, SIDE) for s in quarters]), preferred_element_type=F32)
            for at, s in enumerate(quarters):
                for yh in range(4):
                    beam = row_beam[places[yh]] * col_beam[0:1, s * SIDE : (s + 1) * SIDE]
                    tile = smeared[yh * SIDE : (yh + 1) * SIDE, at * SIDE : (at + 1) * SIDE]
                    csend[s, delta, yh] = (beam * tile * (1.0 / (L * L))).astype(BF)

            @pl.loop(0, 4)
            def _(step):
                yh = lax.rem(yhi + step + 2, 4)
                for s in quarters:
                    yd = 2 * yh + s // 2
                    mine = jnp.logical_and(yd == y, core == s % 2)
                    src = csend.at[s, delta, yh]
                    home = grecv.at[delta, me16]

                    @pl.when(jnp.logical_not(mine))
                    def _():
                        remote(src, home, c_send.at[s], c_recv.at[delta], {"y": yd, "core": s % 2}).start()

                    @pl.when(mine)
                    def _():
                        pltpu.make_async_copy(src, home, c_recv.at[delta]).start()

    back_transform((0,))
    back_transform((1,))
    give_back((0,))
    back_transform((2, 3))
    give_back((1,))
    give_back((2, 3))

    def add_up(delta):
        wait_bytes(grecv.at[delta], c_recv.at[delta])

        @pl.loop(0, 8)
        def _(b):
            rows = pl.ds(b * 16, 16)
            stack = grecv[delta, :, rows, :].reshape(256, SIDE)
            total = jnp.dot(sel[delta], stack, preferred_element_type=F32)
            part[delta, :, rows, :] = total.reshape(16, 16, SIDE)

    def pass_on(step, way, sub, value):
        tiles = slice(2 * sub, 2 * sub + 2)
        k = 2 * step + way
        rss[k, tiles] = value.astype(BF)
        sem = k * SUBS + sub
        copy = remote(rss.at[k, tiles], rsr.at[k, tiles], rs_send.at[sem], rs_recv.at[sem], (up, down)[way])
        copy.start()
        return copy

    def landed(copies, step, way, sub):
        copies[step, way, sub].wait_recv()
        return rsr[2 * step + way, 2 * sub : 2 * sub + 2].astype(F32)

    passed = {}
    classes = [((0, 8), (0, 8)), ((3, 0), (1, 8)), ((2, 0), (2, 8)), ((1, 0), (3, 8))]
    for step in range(4):
        for delta in ((0,), (3, 1), (2,), ())[step]:
            add_up(delta)
        for sub in range(SUBS):
            for way in range(2):
                if step == 0 and sub // 2 != way:
                    continue
                delta, at = classes[step][way]
                value = part[delta, at + 2 * sub : at + 2 * sub + 2]
                if (step - 1, way, sub) in passed:
                    value = value + landed(passed, step - 1, way, sub)
                passed[step, way, sub] = pass_on(step, way, sub, value)

    for copy in started:
        copy.wait_send()
    for delta in range(4):
        wait_bytes(send.at[delta, 0:15], y_send.at[delta])
    for s in range(4):
        wait_bytes(rowsend.at[s, 0:3], x_send.at[s])
        wait_bytes(backsend.at[s, 0:3], b_send.at[s])

        @pl.when(phase == s)
        def _():
            wait_bytes(csend.at[s, :, 0:3], c_send.at[s])

        @pl.when(phase != s)
        def _():
            wait_bytes(csend.at[s], c_send.at[s])

    for way in range(2):
        wait_bytes(xrel.at[way], xf_send.at[way])
    for sub in range(SUBS):
        tiles = slice(2 * sub, 2 * sub + 2)
        out[tiles] = part[0, tiles] + landed(passed, 3, 0, sub) + landed(passed, 3, 1, sub)
    for copy in passed.values():
        copy.wait_send()


def make_shards(table):
    by_rows = table.reshape(PT, SIDE, L)
    by_cols = np.ascontiguousarray(table.reshape(L, PT, SIDE).transpose(1, 0, 2))

    def shards(residual_sky_tiles, cover, beam_width, transfer):
        row_at, col_at = corners(cover, HELD)
        vmem = pl.BlockSpec(memory_space=pltpu.VMEM)
        smem = pl.BlockSpec(memory_space=pltpu.SMEM)
        anywhere = pl.BlockSpec(memory_space=pl.ANY)
        tile = (SIDE, SIDE)
        dma = pltpu.SemaphoreType.DMA
        scratch = [
            pltpu.VMEM((PT, SIDE, L), BF),
            pltpu.VMEM((PT, L, SIDE), BF),
            pltpu.VMEM((SLAB, L), BF),
            pltpu.VMEM((PT,) + tile, F32),
            pltpu.VMEM((8, SLAB), F32),
            pltpu.VMEM((4, 256, 256), BF),
            pltpu.VMEM((17,) + tile, BF),
            pltpu.VMEM((17,) + tile, BF),
            pltpu.VMEM((17,) + tile, BF),
            pltpu.VMEM((17,) + tile, BF),
            pltpu.VMEM((4, 16) + tile, BF),
            pltpu.VMEM((16,) + tile, BF),
            pltpu.VMEM((16,) + tile, BF),
            pltpu.VMEM((16,) + tile, BF),
            pltpu.VMEM((16,) + tile, BF),
            pltpu.VMEM((4, L, SIDE), BF),
            pltpu.VMEM((4, 4, SLAB, SIDE), BF),
            pltpu.VMEM((16, SLAB, SIDE), BF),
            pltpu.VMEM((4, SLAB, SLAB), BF),
            pltpu.VMEM((SLAB, L), F32),
            pltpu.VMEM((SLAB, L), BF),
            pltpu.VMEM((4, 4, SLAB, SIDE), BF),
            pltpu.VMEM((4, 4, SLAB, SIDE), BF),
            pltpu.VMEM((4, 4, 4) + tile, BF),
            pltpu.VMEM((4, 16) + tile, BF),
            pltpu.VMEM((4, 16) + tile, F32),
            pltpu.VMEM((8, 8) + tile, BF),
            pltpu.VMEM((8, 8) + tile, BF),
            pltpu.VMEM((2, 4, 2, HALF, SIDE), BF),
            dma((3,)),
            dma((8 * SUBS,)),
            dma((8 * SUBS,)),
            dma((4,)),
            dma((4, 4)),
            dma((4,)),
            dma((4,)),
            dma((4,)),
            dma((4,)),
            dma((4,)),
            dma((4,)),
            dma((8 * SUBS,)),
            dma((8 * SUBS,)),
            dma((2, 4, 2)),
            dma((2,)),
        ]
        return pl.pallas_call(
            kernel,
            out_shape=jax.ShapeDtypeStruct((HELD,) + tile, F32),
            in_specs=[smem, smem, smem, vmem, anywhere, anywhere, anywhere],
            out_specs=vmem,
            scratch_shapes=scratch,
            compiler_params=pltpu.CompilerParams(
                collective_id=0, has_side_effects=True, vmem_limit_bytes=63 * 1024 * 1024
            ),
            cost_estimate=pl.CostEstimate(flops=4 * 2 * L * L * SLAB, bytes_accessed=20 * 2**20, transcendentals=0),
        )(row_at, col_at, beam_width, residual_sky_tiles, jnp.asarray(by_rows), jnp.asarray(by_cols), transfer)

    return shards


def solution(mesh):
    split = Mesh(mesh.devices.reshape(8, 8, 2, 4), ("z", "y", "core", "fft"))
    over_all = P(("z", "y", "core", "fft"), None, None)
    return jax.shard_map(
        make_shards(hartley_matrix(L)),
        mesh=split,
        in_specs=(over_all, P(), P(), P("fft", None)),
        out_specs=over_all,
        check_vma=False,
    )
```

```python
import math

import jax
import jax.numpy as jnp
import ml_dtypes
import numpy as np
from jax import lax
from jax.experimental import pallas as pl
from jax.experimental.pallas import tpu as pltpu
from jax.sharding import Mesh
from jax.sharding import PartitionSpec as P

PT = 16
ROWS = 64
COLS = 64
SIDE = 128
L = 2048
SLAB = 512
HALF = 256
HELD = 8
SUBS = 4
MESH = pl.DeviceIdType.MESH
BF = jnp.bfloat16
F32 = jnp.float32


def hartley_matrix(length):
    ids = np.arange(length, dtype=np.int64)
    angle = 2.0 * np.pi / length * ((ids[:, None] * ids[None, :]) % length)
    return (np.cos(angle) + np.sin(angle)).astype(np.float32).astype(ml_dtypes.bfloat16)


def corners(cover, tiles_held):
    live = cover >= 0
    holder = cover // tiles_held
    local = cover % tiles_held
    rows = holder // PT + 32 * (local // 4)
    cols = holder % PT + PT * (local % 4)
    position = jnp.arange(PT * PT, dtype=jnp.int32)
    row_at = jnp.max(jnp.where(live, rows - position // PT, -1000), axis=1)
    col_at = jnp.max(jnp.where(live, cols - position % PT, -1000), axis=1)
    return row_at, col_at


def wait_bytes(ref, sem):
    pltpu.make_async_copy(ref, ref, sem).wait()


def kernel(
    row_at, col_at, width, sky, t_hbm, tcol_hbm, transfer_hbm, out,
    tv, tcol, trv, row_beam, col_beam, sel, p0, p1, p2, p3, send, img0, img1, img2, img3, w, rowsend, turned, a, spec, filt,
    backsend, ret, csend, grecv, part, rss, rsr, xrel,
    load_sem, ag_send, ag_recv, y_send, y_recv, x_send, x_recv, b_send, b_recv, c_send, c_recv, rs_send, rs_recv,
    xr_recv, xf_send,
):
    z, y = lax.axis_index("z"), lax.axis_index("y")
    core, x = lax.axis_index("core"), lax.axis_index("fft")
    me16 = y * 2 + core
    yhi = lax.div(y, 2)
    odd = lax.rem(y, 2)
    phase = core + 2 * odd
    col_class = x + 4 * core + 8 * odd
    up = {"z": lax.rem(z + 1, 8)}
    down = {"z": lax.rem(z + 7, 8)}
    pairs = [p0, p1, p2, p3]
    images = [img0, img1, img2, img3]
    order_in = (2, 1, 3, 0)
    turns = (0, 2, 1, 3)

    def remote(src, dst, s_sem, r_sem, where):
        return pltpu.make_async_remote_copy(
            src_ref=src, dst_ref=dst, send_sem=s_sem, recv_sem=r_sem, device_id=where, device_id_type=MESH
        )

    def tile_index(delta, d):
        row, col = row_at[z * 16 + d], col_at[z * 16 + d]
        sky_row = row + lax.rem(yhi + 4 * lax.rem(z + delta, 4) - row + 1024, 16)
        sky_col = col + lax.rem(col_class - col + 1024, 16)
        live = (sky_row >= 0) & (sky_row < ROWS) & (sky_col >= 0) & (sky_col < COLS)
        which = lax.div(lax.rem(lax.div(sky_row, 4) - z - delta + 64, 8), 4)
        return jnp.where(live, which * 8 + lax.div(sky_row, 32) * 4 + lax.div(sky_col, 16), 16)

    load_t = pltpu.make_async_copy(t_hbm, tv, load_sem.at[0])
    load_tr = pltpu.make_async_copy(transfer_hbm, trv, load_sem.at[1])
    load_tcol = pltpu.make_async_copy(tcol_hbm, tcol, load_sem.at[2])

    barrier = pltpu.get_barrier_semaphore()
    pl.semaphore_signal(barrier, inc=1, device_id=up, device_id_type=MESH)
    pl.semaphore_signal(barrier, inc=1, device_id=down, device_id_type=MESH)

    @pl.loop(1, 16)
    def _(step):
        d = lax.rem(me16 + step, 16)
        pl.semaphore_signal(
            barrier, inc=1, device_id={"y": lax.div(d, 2), "core": lax.rem(d, 2)}, device_id_type=MESH
        )

    for step in range(1, 4):
        pl.semaphore_signal(barrier, inc=1, device_id={"fft": lax.rem(x + step, 4)}, device_id_type=MESH)
    load_t.start()
    load_tr.start()
    load_tcol.start()
    p0[0:8] = sky[...].astype(BF)
    for pair in pairs:
        pair[16] = jnp.zeros((SIDE, SIDE), BF)
    pl.semaphore_wait(barrier, 20)

    ring = [
        [(p0.at[0:8], p1.at[0:8], down), (p0.at[0:8], p3.at[8:16], up)],
        [(p1.at[0:8], p2.at[0:8], down), (p3.at[8:16], p2.at[8:16], up)],
        [(p2.at[0:8], p3.at[0:8], down), (p2.at[8:16], p1.at[8:16], up)],
        [(p3.at[0:4], p0.at[8:12], down), (p1.at[12:16], p0.at[12:16], up)],
    ]

    def ring_copy(step, way, sub):
        src, dst, to = ring[step][way]
        part_of = pl.ds(2 * sub if step < 3 else 2 * (sub - 2 * way), 2)
        k = (step * 2 + way) * SUBS + sub
        return remote(src.at[part_of], dst.at[part_of], ag_send.at[k], ag_recv.at[k], to)

    def stage(delta):
        pair = pairs[delta]

        @pl.loop(0, 16)
        def _(d):
            send[delta, d] = pair[tile_index(delta, d)]

    def push(delta, s):
        m = lax.rem(z + delta, 4)
        dst = images[s].at[m * 4 + yhi]
        r_sem = y_recv.at[s, delta]

        @pl.loop(0, 8)
        def _(k):
            offset = 4 + (1 - 2 * lax.rem(k, 2)) * lax.div(k + 1, 2)
            yd = lax.rem(y + offset, 8)
            for c in range(2):
                d = 2 * yd + c

                @pl.when(d != me16)
                def _():
                    remote(send.at[delta, d], dst, y_send.at[delta], r_sem, {"y": yd, "core": c}).start()

        pltpu.make_async_copy(send.at[delta, me16], dst, r_sem).start()

    started = []
    for step in range(4):
        now = []
        for sub in range(SUBS):
            for way in range(2):
                if step > 0:
                    ring_copy(step - 1, way, sub).wait_recv()
                if step < 3 or sub // 2 == way:
                    copy = ring_copy(step, way, sub)
                    copy.start()
                    now.append(copy)
        started += now
        for delta in {2: (2,), 3: (1, 3)}.get(step, ()):
            stage(delta)

            @pl.when(phase == 0)
            def _():
                push(delta, 0)

            if delta == order_in[0]:

                @pl.when(phase == turns[1])
                def _():
                    push(delta, turns[1])

    for copy in now:
        copy.wait_recv()
    stage(0)

    @pl.when(phase == 0)
    def _():
        push(0, 0)

    center = (L - 1) / 2.0
    point = z * 16 + me16
    row_turn = lax.rem(row_at[point] + 1024, 16)
    col_turn = lax.rem(col_at[point] + 1024, 16)
    span = jnp.full((SIDE, SIDE), width[point], F32) * L
    rate = (-4.0 * math.log(2.0)) / (span * span)

    @pl.loop(0, 16)
    def _(i):
        coord = (i * SIDE + lax.broadcasted_iota(jnp.int32, (SIDE, SIDE), 0)).astype(F32) - center
        row_beam[i] = jnp.exp(rate * (coord * coord))

    for s in range(4):
        block = lax.rem(x + 4 * s + 16 - col_turn, 16)
        coord = (block * SIDE + lax.broadcasted_iota(jnp.int32, (8, SIDE), 1)).astype(F32) - center
        col_beam[:, s * SIDE : (s + 1) * SIDE] = jnp.exp(rate[0:8] * (coord * coord))

    @pl.loop(0, 4)
    def _(delta):
        lane = lax.broadcasted_iota(jnp.int32, (8, 256), 1)

        def place(p, acc):
            inside = (lane >= 16 * p) & (lane < 16 * p + 16)
            return jnp.where(inside, tile_index(delta, p) * 16 + lane - 16 * p, acc)

        target = lax.fori_loop(0, 16, place, jnp.zeros((8, 256), jnp.int32))
        row = lax.broadcasted_iota(jnp.int32, (256, 256), 0)
        sel[delta] = jnp.where(row == target[0:1], 1.0, 0.0).astype(BF)

    load_t.wait()
    load_tr.wait()
    load_tcol.wait()

    def wait_chunk(s, delta):
        wait_bytes(images[s].at[0:4], y_recv.at[s, delta])

    def weigh(s):
        image = images[s]

        @pl.loop(0, 16)
        def _(i):
            rc = lax.rem(i + row_turn, 16)
            beam = row_beam[i] * col_beam[0:1, s * SIDE : (s + 1) * SIDE]
            w[s, pl.ds(i * SIDE, SIDE), :] = (beam * image[rc].astype(F32)).astype(BF)

    halves = [slice(0, HALF), slice(HALF, SLAB)]

    def deliver(block, home, stops, s_sem, r_sem, r_sems, rel, xd):
        @pl.when((rel == 1) | (rel == 3))
        def _():
            remote(block, home, s_sem, r_sem, {"fft": xd}).start()

        @pl.when(rel == 2)
        def _():
            for c in range(2):
                to = {"fft": lax.rem(x + 1 + 2 * c, 4)}
                remote(block.at[halves[c]], stops[c], s_sem, r_sems.at[c], to).start()

        @pl.when(rel == 0)
        def _():
            pltpu.make_async_copy(block, home, r_sem).start()

    def pass_blocks(stops, homes, f_sem, r_sem, r_sems):
        for c in range(2):
            wait_bytes(stops[c], r_sems.at[c])
            home = homes[c].at[halves[c]]
            remote(stops[c], home, f_sem, r_sem, {"fft": lax.rem(x + 1 + 2 * c, 4)}).start()

    sources = [lax.rem(x + 3 - 2 * c, 4) for c in range(2)]

    def row_transform(s):
        stops = [xrel.at[0, s, c] for c in range(2)]

        @pl.loop(0, 4)
        def _(t):
            rel = lax.rem(2 + t + lax.div(t, 2) + 2 * lax.div(t, 3), 4)
            xd = lax.rem(x + rel, 4)
            slab = jnp.dot(tv[pl.ds(xd * 4, 4)].reshape(SLAB, L), w[s], preferred_element_type=F32)
            rowsend[s, xd] = slab.astype(BF)
            deliver(
                rowsend.at[s, xd], turned.at[x + 4 * s], stops, x_send.at[s], x_recv.at[s], xr_recv.at[0, s], rel, xd
            )

        homes = [turned.at[source + 4 * s] for source in sources]
        pass_blocks(stops, homes, xf_send.at[0], x_recv.at[s], xr_recv.at[0, s])

    def add_spectrum(s):
        wait_bytes(turned.at[4 * s : 4 * s + 4], x_recv.at[s])
        for k in range(4):
            a[s, :, k * SIDE : (k + 1) * SIDE] = turned[4 * s + k]
        places = [lax.rem(4 * s + k + 16 - col_turn, 16) for k in range(4)]
        for n in range(4):
            cols = slice(n * SLAB, (n + 1) * SLAB)
            rhs = jnp.concatenate([tv[j, :, cols] for j in places], axis=0)
            total = jnp.dot(a[s], rhs, preferred_element_type=F32)
            if s > 0:
                total = spec[:, cols] + total
            if s < 3:
                spec[:, cols] = total
            else:
                filt[:, cols] = (trv[:, cols].astype(F32) * total.astype(BF).astype(F32)).astype(BF)

    for number, s in enumerate(turns):
        later = turns[number + 1] if number < 3 else None
        for at, delta in enumerate(order_in):
            if later is not None and at > (1 if number == 0 else 0):

                @pl.when(phase == later)
                def _():
                    push(order_in[at - 1], later)

            wait_chunk(s, delta)
        if later is not None:

            @pl.when(phase == later)
            def _():
                push(order_in[3], later)

        weigh(s)
        row_transform(s)
        if number > 0:
            add_spectrum(turns[number - 1])
    add_spectrum(3)

    def back_transform(s):
        stops = [xrel.at[1, s, c] for c in range(2)]

        @pl.loop(0, 4)
        def _(t):
            rel = lax.rem(2 + t + lax.div(t, 2) + 2 * lax.div(t, 3), 4)
            xd = lax.rem(x + rel, 4)
            picked = tcol[lax.rem(xd + 4 * s + 16 - col_turn, 16)]
            backsend[s, xd] = jnp.dot(filt[...], picked, preferred_element_type=F32).astype(BF)
            deliver(
                backsend.at[s, xd], ret.at[s, x], stops, b_send.at[s], b_recv.at[s], xr_recv.at[1, s], rel, xd
            )

        homes = [ret.at[s, source] for source in sources]
        pass_blocks(stops, homes, xf_send.at[1], b_recv.at[s], xr_recv.at[1, s])

    def give_back(s):
        wait_bytes(ret.at[s], b_recv.at[s])

        @pl.loop(0, 4)
        def _(turn):
            delta = turn + lax.div(turn, 2) * (5 - 2 * turn)
            m = lax.rem(z + delta, 4)
            places = [lax.rem(4 * m + yh + 16 - row_turn, 16) for yh in range(4)]
            lhs = jnp.concatenate([tv[i] for i in places], axis=0)
            smeared = jnp.dot(lhs, ret[s].reshape(L, SIDE), preferred_element_type=F32)
            for yh in range(4):
                beam = row_beam[places[yh]] * col_beam[0:1, s * SIDE : (s + 1) * SIDE]
                tile = smeared[yh * SIDE : (yh + 1) * SIDE]
                csend[s, delta, yh] = (beam * tile * (1.0 / (L * L))).astype(BF)

            @pl.loop(0, 4)
            def _(step):
                yh = lax.rem(yhi + step + 2, 4)
                yd = 2 * yh + s // 2
                mine = jnp.logical_and(yd == y, core == s % 2)
                src = csend.at[s, delta, yh]
                home = grecv.at[delta, me16]

                @pl.when(jnp.logical_not(mine))
                def _():
                    remote(src, home, c_send.at[s], c_recv.at[delta], {"y": yd, "core": s % 2}).start()

                @pl.when(mine)
                def _():
                    pltpu.make_async_copy(src, home, c_recv.at[delta]).start()

    back_transform(turns[0])
    back_transform(turns[1])
    give_back(turns[0])
    back_transform(turns[2])
    give_back(turns[1])
    back_transform(turns[3])
    give_back(turns[2])
    give_back(turns[3])

    def add_up(delta):
        wait_bytes(grecv.at[delta], c_recv.at[delta])

        @pl.loop(0, 8)
        def _(b):
            rows = pl.ds(b * 16, 16)
            stack = grecv[delta, :, rows, :].reshape(256, SIDE)
            total = jnp.dot(sel[delta], stack, preferred_element_type=F32)
            part[delta, :, rows, :] = total.reshape(16, 16, SIDE)

    def pass_on(step, way, sub, value):
        tiles = slice(2 * sub, 2 * sub + 2)
        k = 2 * step + way
        rss[k, tiles] = value.astype(BF)
        sem = k * SUBS + sub
        copy = remote(rss.at[k, tiles], rsr.at[k, tiles], rs_send.at[sem], rs_recv.at[sem], (up, down)[way])
        copy.start()
        return copy

    def landed(copies, step, way, sub):
        copies[step, way, sub].wait_recv()
        return rsr[2 * step + way, 2 * sub : 2 * sub + 2].astype(F32)

    passed = {}
    classes = [((0, 8), (0, 8)), ((3, 0), (1, 8)), ((2, 0), (2, 8)), ((1, 0), (3, 8))]
    for step in range(4):
        for delta in ((0,), (3, 1), (2,), ())[step]:
            add_up(delta)
        for sub in range(SUBS):
            for way in range(2):
                if step == 0 and sub // 2 != way:
                    continue
                delta, at = classes[step][way]
                value = part[delta, at + 2 * sub : at + 2 * sub + 2]
                if (step - 1, way, sub) in passed:
                    value = value + landed(passed, step - 1, way, sub)
                passed[step, way, sub] = pass_on(step, way, sub, value)

    for copy in started:
        copy.wait_send()
    for delta in range(4):
        wait_bytes(send.at[delta, 0:15], y_send.at[delta])
    for s in range(4):
        wait_bytes(rowsend.at[s, 0:3], x_send.at[s])
        wait_bytes(backsend.at[s, 0:3], b_send.at[s])

        @pl.when(phase == s)
        def _():
            wait_bytes(csend.at[s, :, 0:3], c_send.at[s])

        @pl.when(phase != s)
        def _():
            wait_bytes(csend.at[s], c_send.at[s])

    for way in range(2):
        wait_bytes(xrel.at[way], xf_send.at[way])
    for sub in range(SUBS):
        tiles = slice(2 * sub, 2 * sub + 2)
        out[tiles] = part[0, tiles] + landed(passed, 3, 0, sub) + landed(passed, 3, 1, sub)
    for copy in passed.values():
        copy.wait_send()


def make_shards(table):
    by_rows = table.reshape(PT, SIDE, L)
    by_cols = np.ascontiguousarray(table.reshape(L, PT, SIDE).transpose(1, 0, 2))

    def shards(residual_sky_tiles, cover, beam_width, transfer):
        row_at, col_at = corners(cover, HELD)
        vmem = pl.BlockSpec(memory_space=pltpu.VMEM)
        smem = pl.BlockSpec(memory_space=pltpu.SMEM)
        anywhere = pl.BlockSpec(memory_space=pl.ANY)
        tile = (SIDE, SIDE)
        dma = pltpu.SemaphoreType.DMA
        scratch = [
            pltpu.VMEM((PT, SIDE, L), BF),
            pltpu.VMEM((PT, L, SIDE), BF),
            pltpu.VMEM((SLAB, L), BF),
            pltpu.VMEM((PT,) + tile, F32),
            pltpu.VMEM((8, SLAB), F32),
            pltpu.VMEM((4, 256, 256), BF),
            pltpu.VMEM((17,) + tile, BF),
            pltpu.VMEM((17,) + tile, BF),
            pltpu.VMEM((17,) + tile, BF),
            pltpu.VMEM((17,) + tile, BF),
            pltpu.VMEM((4, 16) + tile, BF),
            pltpu.VMEM((16,) + tile, BF),
            pltpu.VMEM((16,) + tile, BF),
            pltpu.VMEM((16,) + tile, BF),
            pltpu.VMEM((16,) + tile, BF),
            pltpu.VMEM((4, L, SIDE), BF),
            pltpu.VMEM((4, 4, SLAB, SIDE), BF),
            pltpu.VMEM((16, SLAB, SIDE), BF),
            pltpu.VMEM((4, SLAB, SLAB), BF),
            pltpu.VMEM((SLAB, L), F32),
            pltpu.VMEM((SLAB, L), BF),
            pltpu.VMEM((4, 4, SLAB, SIDE), BF),
            pltpu.VMEM((4, 4, SLAB, SIDE), BF),
            pltpu.VMEM((4, 4, 4) + tile, BF),
            pltpu.VMEM((4, 16) + tile, BF),
            pltpu.VMEM((4, 16) + tile, F32),
            pltpu.VMEM((8, 8) + tile, BF),
            pltpu.VMEM((8, 8) + tile, BF),
            pltpu.VMEM((2, 4, 2, HALF, SIDE), BF),
            dma((3,)),
            dma((8 * SUBS,)),
            dma((8 * SUBS,)),
            dma((4,)),
            dma((4, 4)),
            dma((4,)),
            dma((4,)),
            dma((4,)),
            dma((4,)),
            dma((4,)),
            dma((4,)),
            dma((8 * SUBS,)),
            dma((8 * SUBS,)),
            dma((2, 4, 2)),
            dma((2,)),
        ]
        return pl.pallas_call(
            kernel,
            out_shape=jax.ShapeDtypeStruct((HELD,) + tile, F32),
            in_specs=[smem, smem, smem, vmem, anywhere, anywhere, anywhere],
            out_specs=vmem,
            scratch_shapes=scratch,
            compiler_params=pltpu.CompilerParams(
                collective_id=0, has_side_effects=True, vmem_limit_bytes=63 * 1024 * 1024
            ),
            cost_estimate=pl.CostEstimate(flops=4 * 2 * L * L * SLAB, bytes_accessed=20 * 2**20, transcendentals=0),
        )(row_at, col_at, beam_width, residual_sky_tiles, jnp.asarray(by_rows), jnp.asarray(by_cols), transfer)

    return shards


def solution(mesh):
    split = Mesh(mesh.devices.reshape(8, 8, 2, 4), ("z", "y", "core", "fft"))
    over_all = P(("z", "y", "core", "fft"), None, None)
    return jax.shard_map(
        make_shards(hartley_matrix(L)),
        mesh=split,
        in_specs=(over_all, P(), P(), P("fft", None)),
        out_specs=over_all,
        check_vma=False,
    )
```
